32 devices in a mesh: parts: 2 (over y), tensor: 4 (over x, core), request: 4 (over z).
Axes of the slice: x: 2, y: 2, z: 4, core: 2. Of those that a mesh axis runs over, the one named last changes fastest.
Arguments:
- attn_heads: bfloat16 [768, 8192], P('parts', 'tensor'), parts along dimension 0, may hold values from -6 to 6
- out_weight: bfloat16 [8192, 8192], P('tensor', 'request'), may hold values from -0.0625 to 0.0625
- resid: bfloat16 [768, 8192], P(('parts', 'tensor'), 'request'), parts along dimension 0
- gain: bfloat16 [8192], P('request'), may hold values from 0.5 to 1.5
- gate_weight: bfloat16 [8192, 14336], P('request', 'tensor'), may hold values from -0.0625 to 0.0625
- up_weight: bfloat16 [8192, 14336], P('request', 'tensor'), may hold values from -0.0625 to 0.0625
- down_weight: bfloat16 [14336, 8192], P('tensor', 'request'), may hold values from -0.046875 to 0.046875
- signs: int32 [4, 8192], P(None, 'request'), may hold values from 0 to 1
- expos: int32 [4, 64], P(None, 'request'), may hold values from -12 to -8
Outputs:
- mixed: bfloat16 [768, 8192], P('parts', 'request'), parts along dimension 0
The draws below stay inside these ranges and needn't reach their ends.
There are 2 independent parts, one for each index of `parts`. The reference program is written for one: setup_inputs(seed, part) draws one part's arguments, and reference() takes and returns one part's arrays. A program takes and returns all parts, laid end to end along the dimension named above; an argument that names none is the same for every part. Nothing has to cross between parts.
Inputs may be any that keep to these rules, and one draw needn't show every extreme that they name: `signs`: each entry is 0 or 1 and stands for the sign 2 s - 1.
All inputs are finite; a program needn't handle non-finite values.
Results may differ from the reference program's by a relative error of at most 0.013.
Values may be sent and summed in bfloat16 or wider, within the bound.
A program may use at most 192 MiB of HBM per device.

```python
import jax
import jax.numpy as jnp
from jax import lax

D = 8192
HEADS = 64
HEAD_DIM = 128
FF = 14336
REQ = 384
N_TENSOR = 4


def draw_resid(key, part):
    key = jax.random.fold_in(key, 5)
    first = jax.random.fold_in(key, 0)
    ramp = 1.0 + 2.0 * jnp.arange(D, dtype=jnp.float32) / (D - 1)
    base = jax.random.normal(first, (REQ, D), jnp.float32)
    return (base * ramp[None, :]).astype(jnp.bfloat16)


def with_ends(values, rng, least, largest):
    spot = [jax.random.randint(jax.random.fold_in(rng, axis), (), 0, length) for axis, length in enumerate(values.shape)]
    longest = values.shape.index(max(values.shape))
    next_to = spot[:longest] + [(spot[longest] + 1) % values.shape[longest]] + spot[longest + 1:]
    return values.at[tuple(spot)].set(least).at[tuple(next_to)].set(largest)


def spiked(values, key, source, target, parts, factor):
    def block_of(dim):
        return (jnp.arange(values.shape[dim]) // (values.shape[dim] // parts)).reshape((-1,) + (1,) * (values.ndim - 1 - dim))

    first = jax.random.permutation(key, parts)[block_of(target)]
    far = (block_of(target) + parts // 2) % parts
    return jnp.where((block_of(source) == first) | (block_of(source) == far), factor * values, values)


def levels(stream_key, dims, shards, smallest, largest):
    def one(dim, blocks):
        heights = jax.random.uniform(jax.random.fold_in(jax.random.fold_in(stream_key, 6), dim), (blocks,), jnp.float32, smallest / len(shards), largest / len(shards))
        return jnp.repeat(jnp.exp(heights), dims[dim] // blocks).reshape((-1,) + (1,) * (len(dims) - dim - 1))

    level = one(*shards[0])
    for cut in shards[1:]:
        level = level * one(*cut)
    return level


def centred(key, extent, spread, most, cuts=(), kind=jnp.bfloat16):
    result = jax.random.normal(key, extent, jnp.float32) * spread
    if len(cuts) > 0:
        result = levels(key, extent, cuts, -0.22, 0.18) * result
    return jnp.clip(result, min=-most, max=most).astype(kind)


def noise_with(key, shape, width, bound, cuts, heavy, kind=jnp.bfloat16):
    entries = width * jax.random.normal(key, shape, jnp.float32)
    if cuts:
        entries = entries * levels(key, shape, cuts, -0.22, 0.18)
    return jnp.clip(spiked(entries, jax.random.fold_in(key, 3), *heavy), -bound, bound).astype(kind)


def setup_inputs(seed: int = 0, part: int = 0) -> dict:
    key_list = jax.random.split(jax.random.key(seed), 10)
    part_keys = jax.random.split(jax.random.fold_in(key_list[9], part), 10)
    attn_heads = noise_with(part_keys[0], (REQ, HEADS * HEAD_DIM), 1.0, 6.0, ((1, 4),), (1, 0, 4, 2.0))
    out_weight = centred(key_list[1], (HEADS * HEAD_DIM, D), (HEADS * HEAD_DIM) ** -0.5, 0.0625, ((0, 4), (1, 4)))
    resid = draw_resid(jax.random.fold_in(jax.random.fold_in(key_list[9], part), 71), part)
    gain = jnp.clip(1.0 + 0.1 * jax.random.normal(key_list[3], (D,), jnp.float32), 0.5, 1.5).astype(jnp.bfloat16)
    gate_weight = centred(key_list[4], (D, FF), D ** -0.5, 0.0625, ((0, 4), (1, 4)))
    up_weight = centred(key_list[5], (D, FF), D ** -0.5, 0.0625, ((0, 4), (1, 4)))
    down_weight = centred(key_list[6], (FF, D), FF ** -0.5, 0.046875, ((0, 4), (1, 4)))
    signs = with_ends(jax.random.randint(key_list[7], (4, D), 0, 2), jax.random.fold_in(key_list[7], 1), 0, 1).astype(jnp.int32)
    expos = with_ends(jax.random.randint(key_list[8], (4, D // 128), -12, -7), jax.random.fold_in(key_list[8], 1), -12, (-7) - 1).astype(jnp.int32)
    return {"attn_heads": attn_heads, "out_weight": out_weight, "resid": resid, "gain": gain, "gate_weight": gate_weight, "up_weight": up_weight, "down_weight": down_weight, "signs": signs, "expos": expos}


def hadamard():
    index = jnp.arange(128, dtype=jnp.int32)
    common = jnp.bitwise_and(index[:, None], index[None, :])
    ones_count = jnp.zeros((128, 128), jnp.int32)
    for level in range(7):
        ones_count = ones_count + jnp.bitwise_and(jnp.right_shift(common, level), 1)
    return (1 - 2 * (ones_count % 2)).astype(jnp.float32)

def rotate(values, sign_bits):
    shape = values.shape
    flipped = values * (2 * sign_bits - 1).astype(jnp.float32)
    turned = jnp.dot(flipped.reshape(-1, 128), hadamard(), precision=lax.Precision.HIGHEST)
    return turned.reshape(shape) * 0.125

def unrotate(values, sign_bits):
    shape = values.shape
    turned = jnp.dot(values.reshape(-1, 128), hadamard(), precision=lax.Precision.HIGHEST)
    return turned.reshape(shape) * 0.0625 * (2 * sign_bits - 1).astype(jnp.float32)

def encode(values, sign_bits, exponents, offset):
    factor = jnp.repeat(jnp.exp2(-(exponents + offset).astype(jnp.float32)), 128)
    return jnp.clip(rotate(values, sign_bits) * factor, -448.0, 448.0).astype(jnp.bfloat16)

def decode(values, sign_bits, exponents, offset):
    factor = jnp.repeat(jnp.exp2((exponents + offset).astype(jnp.float32)), 128)
    return unrotate(values * factor, sign_bits)

def reference(attn_heads, out_weight, resid, gain, gate_weight, up_weight, down_weight, signs, expos):
    groups = N_TENSOR
    head_rows = HEADS * HEAD_DIM // groups
    left = attn_heads.astype(jnp.float32).reshape(REQ, groups, head_rows)
    right = out_weight.astype(jnp.float32).reshape(groups, head_rows, D)
    terms = jnp.einsum('rgk,gkd->grd', left, right, precision=lax.Precision.HIGHEST)
    coded = encode(terms.reshape(groups * REQ, D), signs[0], expos[0], 4)
    total = lax.optimization_barrier(jnp.sum(coded.astype(jnp.float32).reshape(groups, REQ, D), axis=0))
    hidden_state = resid.astype(jnp.float32) + decode(total, signs[0], expos[0], 4)
    restored = decode(encode(hidden_state, signs[1], expos[1], 8).astype(jnp.float32), signs[1], expos[1], 8)
    square_sum = lax.optimization_barrier(jnp.sum(restored * restored, axis=1))
    normed = (restored * gain.astype(jnp.float32)).astype(jnp.bfloat16)
    factor = lax.rsqrt(square_sum / D + 1e-05)[:, None]
    gate = factor * jnp.dot(normed, gate_weight, preferred_element_type=jnp.float32)
    up = factor * jnp.dot(normed, up_weight, preferred_element_type=jnp.float32)
    hidden = (jax.nn.silu(gate) * up).astype(jnp.bfloat16)
    unit_rows = FF // groups
    left_ffn = hidden.astype(jnp.float32).reshape(REQ, groups, unit_rows)
    right_ffn = down_weight.astype(jnp.float32).reshape(groups, unit_rows, D)
    ffn_terms = jnp.einsum('rgk,gkd->grd', left_ffn, right_ffn, precision=lax.Precision.HIGHEST)
    coded_ffn = encode(ffn_terms.reshape(groups * REQ, D), signs[2], expos[2], 4)
    ffn_total = lax.optimization_barrier(jnp.sum(coded_ffn.astype(jnp.float32).reshape(groups, REQ, D), axis=0))
    updated = hidden_state + decode(ffn_total, signs[2], expos[2], 4)
    final_code = encode(updated, signs[3], expos[3], 6).astype(jnp.float32)
    return decode(final_code, signs[3], expos[3], 6).astype(jnp.bfloat16)
```

```python
import functools

import jax
import jax.numpy as jnp
from jax import lax
from jax.experimental import pallas as pl
from jax.experimental.pallas import tpu as pltpu
from jax.sharding import PartitionSpec as P

D = 8192
MESH = pl.DeviceIdType.MESH
LAG = 2
VMEM_LIMIT = 52 * 2**20


def hadamard():
    index = jnp.arange(128, dtype=jnp.int32)
    common = jnp.bitwise_and(index[:, None], index[None, :])
    ones_count = jnp.zeros((128, 128), jnp.int32)
    for level in range(7):
        ones_count = ones_count + jnp.bitwise_and(jnp.right_shift(common, level), 1)
    return (1 - 2 * (ones_count % 2)).astype(jnp.bfloat16)


def turn(values, had):
    high = values.astype(jnp.bfloat16)
    low = (values - high.astype(jnp.float32)).astype(jnp.bfloat16)
    return jnp.dot(high, had, preferred_element_type=jnp.float32) + jnp.dot(low, had, preferred_element_type=jnp.float32)


def encode(values, sign, scale, had):
    return jnp.clip(turn(values * sign, had) * scale, -448.0, 448.0).astype(jnp.bfloat16)


def decode(codes, scale, had):
    return jnp.dot(codes, had, preferred_element_type=jnp.float32) * scale


def project_body(a_ref, w_ref, sign_ref, scale_ref, had_ref, o_ref):
    product = jnp.dot(a_ref[...], w_ref[...], preferred_element_type=jnp.float32)
    for low in range(0, product.shape[1], 128):
        cols = slice(low, low + 128)
        o_ref[:, cols] = encode(product[:, cols], sign_ref[:, cols], scale_ref[:, cols], had_ref[...])


def project(a, w, sign, scale, had):
    rows, depth = a.shape
    width = w.shape[1]
    block = 256
    return pl.pallas_call(
        project_body,
        grid=(width // block,),
        in_specs=[
            pl.BlockSpec((rows, depth), lambda j: (0, 0)),
            pl.BlockSpec((depth, block), lambda j: (0, j)),
            pl.BlockSpec((1, block), lambda j: (0, j)),
            pl.BlockSpec((1, block), lambda j: (0, j)),
            pl.BlockSpec((128, 128), lambda j: (0, 0)),
        ],
        out_specs=pl.BlockSpec((rows, block), lambda j: (0, j)),
        out_shape=jax.ShapeDtypeStruct((rows, width), jnp.bfloat16),
        compiler_params=pltpu.CompilerParams(vmem_limit_bytes=VMEM_LIMIT),
    )(a, w, sign, scale, had)


def recode_body(code_ref, base_ref, dec_ref, sign_ref, scale_ref, had_ref, state_ref, o_ref):
    for low in range(0, code_ref.shape[1], 128):
        cols = slice(low, low + 128)
        state = base_ref[:, cols].astype(jnp.float32) + decode(code_ref[:, cols], dec_ref[:, cols], had_ref[...])
        state_ref[:, cols] = state
        o_ref[:, cols] = encode(state, sign_ref[:, cols], scale_ref[:, cols], had_ref[...])


def recode(code, base, dec, sign, scale, had):
    return pl.pallas_call(
        recode_body,
        out_shape=(jax.ShapeDtypeStruct(code.shape, jnp.float32), jax.ShapeDtypeStruct(code.shape, jnp.bfloat16)),
        compiler_params=pltpu.CompilerParams(vmem_limit_bytes=VMEM_LIMIT),
    )(code, base, dec, sign, scale, had)


def finish_body(code_ref, dec_ref, had_ref, o_ref):
    for low in range(0, code_ref.shape[1], 128):
        cols = slice(low, low + 128)
        o_ref[:, cols] = decode(code_ref[:, cols], dec_ref[:, cols], had_ref[...]).astype(jnp.bfloat16)


def finish(code, dec, had):
    rows, width = code.shape
    block = min(width, 512)
    return pl.pallas_call(
        finish_body,
        grid=(width // block,),
        in_specs=[
            pl.BlockSpec((rows, block), lambda j: (0, j)),
            pl.BlockSpec((1, block), lambda j: (0, j)),
            pl.BlockSpec((128, 128), lambda j: (0, 0)),
        ],
        out_specs=pl.BlockSpec((rows, block), lambda j: (0, j)),
        out_shape=jax.ShapeDtypeStruct((rows, width), jnp.bfloat16),
        compiler_params=pltpu.CompilerParams(vmem_limit_bytes=VMEM_LIMIT),
    )(code, dec, had)


def ffn_body(n, chunks, cw, code_ref, dec_ref, gain_ref, had_ref, gate_ref, up_ref, h_ref,
             x_ref, sq_ref, sqr_ref, w_ref, p_ref, r_ref,
             w_sem, rs_send, rs_recv, ag_send, ag_recv, sq_send, sq_recv):
    z = lax.axis_index("request")
    half = p_ref.shape[2]

    def weights(c, slot):
        cols = pl.ds(pl.multiple_of(c * cw, cw), cw)
        return (
            pltpu.make_async_copy(gate_ref.at[:, cols], w_ref.at[slot, :, pl.ds(0, cw)], w_sem.at[slot, 0]),
            pltpu.make_async_copy(up_ref.at[:, cols], w_ref.at[slot, :, pl.ds(cw, cw)], w_sem.at[slot, 1]),
        )

    barrier = pltpu.get_barrier_semaphore()

    @pl.when(z > 0)
    def _():
        pl.semaphore_signal(barrier, inc=1, device_id={"request": z - 1}, device_id_type=MESH)

    @pl.when(z < n - 1)
    def _():
        pl.semaphore_signal(barrier, inc=1, device_id={"request": z + 1}, device_id_type=MESH)

    for copy in weights(0, 0):
        copy.start()

    sq_ref[...] = jnp.zeros_like(sq_ref)

    @pl.loop(0, code_ref.shape[1] // 128)
    def _(b):
        cols = pl.ds(pl.multiple_of(b * 128, 128), 128)
        restored = decode(code_ref[:, cols], dec_ref[:, cols], had_ref[...])
        squared = restored * restored
        sq_ref[0] += squared[:half]
        sq_ref[1] += squared[half:]
        x_ref[:, cols] = (restored * gain_ref[:, cols]).astype(jnp.bfloat16)

    pl.semaphore_wait(barrier, (z > 0).astype(jnp.int32) + (z < n - 1).astype(jnp.int32))

    place = (n - 1 - z, z)
    after = (z - 1, z + 1)
    before = (z + 1, z - 1)

    def sum_copy(d, c):
        return pltpu.make_async_remote_copy(
            src_ref=p_ref.at[d, c], dst_ref=r_ref.at[d, c], send_sem=rs_send.at[d, c], recv_sem=rs_recv.at[d, c],
            device_id={"request": after[d]}, device_id_type=MESH)

    def square_copy(d):
        return pltpu.make_async_remote_copy(
            src_ref=sq_ref.at[d], dst_ref=sqr_ref.at[d], send_sem=sq_send.at[d], recv_sem=sq_recv.at[d],
            device_id={"request": after[d]}, device_id_type=MESH)

    def hidden_copy(d, c):
        part = h_ref.at[pl.ds(d * half, half), pl.ds(pl.multiple_of(c * cw, cw), cw)]
        return pltpu.make_async_remote_copy(
            src_ref=part, dst_ref=part, send_sem=ag_send.at[d, c], recv_sem=ag_recv.at[d, c],
            device_id={"request": before[d]}, device_id_type=MESH)

    @pl.loop(0, chunks + 2 * (n - 1) * LAG)
    def _(s):
        @pl.when(s < chunks)
        def _():
            slot = lax.rem(s, 2)

            @pl.when(s + 1 < chunks)
            def _():
                for copy in weights(s + 1, 1 - slot):
                    copy.start()

            for copy in weights(s, slot):
                copy.wait()
            total = jnp.dot(x_ref[...], w_ref[slot], preferred_element_type=jnp.float32).astype(jnp.bfloat16)
            p_ref[0, s] = total[:half]
            p_ref[1, s] = total[half:]

        for d in (0, 1):
            pos = place[d]
            c = s - pos * LAG

            @pl.when((c >= 0) & (c < chunks))
            def _(d=d, pos=pos, c=c):
                @pl.when(c == 0)
                def _():
                    @pl.when(pos > 0)
                    def _():
                        square_copy(d).wait_recv()
                        sq_ref[d] += sqr_ref[d]

                    @pl.when(pos < n - 1)
                    def _():
                        square_copy(d).start()

                    @pl.when(pos == n - 1)
                    def _():
                        total = jnp.sum(sq_ref[d], axis=1, keepdims=True)
                        sq_ref[d] = jnp.broadcast_to(lax.rsqrt(total / D + 1e-05), sq_ref.shape[1:])

                @pl.when(pos > 0)
                def _():
                    sum_copy(d, c).wait_recv()
                    p_ref[d, c] = (p_ref[d, c].astype(jnp.float32) + r_ref[d, c].astype(jnp.float32)).astype(jnp.bfloat16)

                @pl.when(pos < n - 1)
                def _():
                    sum_copy(d, c).start()

                @pl.when(pos == n - 1)
                def _():
                    cols = pl.multiple_of(c * cw, cw)
                    for low in range(0, cw, 128):
                        factor = sq_ref[d]
                        gate = p_ref[d, c, :, low:low + 128].astype(jnp.float32) * factor
                        up = p_ref[d, c, :, cw + low:cw + low + 128].astype(jnp.float32) * factor
                        value = gate / (1.0 + jnp.exp(-gate)) * up
                        h_ref[pl.ds(d * half, half), pl.ds(pl.multiple_of(cols + low, 128), 128)] = value.astype(jnp.bfloat16)
                    hidden_copy(d, c).start()

            back = s - (2 * (n - 1) - pos) * LAG

            @pl.when((pos < n - 1) & (back >= 0) & (back < chunks))
            def _(d=d, pos=pos, back=back):
                hidden_copy(d, back).wait_recv()

                @pl.when(pos > 0)
                def _():
                    hidden_copy(d, back).start()

    for d in (0, 1):
        pos = place[d]

        @pl.when(pos < n - 1)
        def _(d=d):
            square_copy(d).wait_send()

            @pl.loop(0, chunks)
            def _(c):
                sum_copy(d, c).wait_send()

        @pl.when(pos > 0)
        def _(d=d):
            @pl.loop(0, chunks)
            def _(c):
                hidden_copy(d, c).wait_send()


def ffn(n, code, dec, gain, had, gate_weight, up_weight):
    rows, depth = code.shape
    units = gate_weight.shape[1]
    cw = 128
    chunks = units // cw
    half = rows // 2
    vmem = pl.BlockSpec(memory_space=pltpu.VMEM)
    return pl.pallas_call(
        functools.partial(ffn_body, n, chunks, cw),
        out_shape=jax.ShapeDtypeStruct((rows, units), jnp.bfloat16),
        in_specs=[vmem] * 4 + [pl.BlockSpec(memory_space=pl.ANY)] * 2,
        out_specs=vmem,
        scratch_shapes=[
            pltpu.VMEM((rows, depth), jnp.bfloat16),
            pltpu.VMEM((2, half, 128), jnp.float32),
            pltpu.VMEM((2, half, 128), jnp.float32),
            pltpu.VMEM((2, depth, 2 * cw), jnp.bfloat16),
            pltpu.VMEM((2, chunks, half, 2 * cw), jnp.bfloat16),
            pltpu.VMEM((2, chunks, half, 2 * cw), jnp.bfloat16),
            pltpu.SemaphoreType.DMA((2, 2)),
            pltpu.SemaphoreType.DMA((2, chunks)),
            pltpu.SemaphoreType.DMA((2, chunks)),
            pltpu.SemaphoreType.DMA((2, chunks)),
            pltpu.SemaphoreType.DMA((2, chunks)),
            pltpu.SemaphoreType.DMA((2,)),
            pltpu.SemaphoreType.DMA((2,)),
        ],
        compiler_params=pltpu.CompilerParams(collective_id=0, has_side_effects=True, vmem_limit_bytes=VMEM_LIMIT),
    )(code, dec, gain, had, gate_weight, up_weight)


def shards(n_request, attn_heads, out_weight, resid, gain, gate_weight, up_weight, down_weight, signs, expos):
    had = hadamard()
    sign = (2 * signs - 1).astype(jnp.float32)
    shift = expos + jnp.array([[4], [8], [4], [6]], jnp.int32)
    enc = jnp.repeat(0.125 * jnp.exp2(-shift.astype(jnp.float32)), 128, axis=1)
    dec = jnp.repeat(0.0625 * jnp.exp2(shift.astype(jnp.float32)), 128, axis=1) * sign
    row = lambda table, k: table[k:k + 1]

    coded = project(attn_heads, out_weight, row(sign, 0), row(enc, 0), had)
    summed = lax.psum_scatter(coded, "tensor", scatter_dimension=0, tiled=True)
    hidden_state, coded = recode(summed, resid, row(dec, 0), row(sign, 1), row(enc, 1), had)
    gathered = lax.all_gather(coded, "tensor", axis=0, tiled=True)
    hidden = ffn(n_request, gathered, row(dec, 1), gain.astype(jnp.float32)[None, :], had, gate_weight, up_weight)
    coded = project(hidden, down_weight, row(sign, 2), row(enc, 2), had)
    summed = lax.psum_scatter(coded, "tensor", scatter_dimension=0, tiled=True)
    _, coded = recode(summed, hidden_state, row(dec, 2), row(sign, 3), row(enc, 3), had)
    gathered = lax.all_gather(coded, "tensor", axis=0, tiled=True)
    return finish(gathered, row(dec, 3), had)


def solution(mesh):
    return jax.shard_map(
        functools.partial(shards, mesh.shape["request"]),
        mesh=mesh,
        in_specs=(
            P("parts", "tensor"),
            P("tensor", "request"),
            P(("parts", "tensor"), "request"),
            P("request"),
            P("request", "tensor"),
            P("request", "tensor"),
            P("tensor", "request"),
            P(None, "request"),
            P(None, "request"),
        ),
        out_specs=P("parts", "request"),
        check_vma=False,
    )
```

```python
import functools

import jax
import jax.numpy as jnp
from jax import lax
from jax.experimental import pallas as pl
from jax.experimental.pallas import tpu as pltpu
from jax.sharding import PartitionSpec as P

D = 8192
MESH = pl.DeviceIdType.MESH
LAG = 2
VMEM_LIMIT = 52 * 2**20


def hadamard():
    index = jnp.arange(128, dtype=jnp.int32)
    common = jnp.bitwise_and(index[:, None], index[None, :])
    ones_count = jnp.zeros((128, 128), jnp.int32)
    for level in range(7):
        ones_count = ones_count + jnp.bitwise_and(jnp.right_shift(common, level), 1)
    return (1 - 2 * (ones_count % 2)).astype(jnp.bfloat16)


def turn(values, had):
    high = values.astype(jnp.bfloat16)
    low = (values - high.astype(jnp.float32)).astype(jnp.bfloat16)
    return jnp.dot(high, had, preferred_element_type=jnp.float32) + jnp.dot(low, had, preferred_element_type=jnp.float32)


def encode(values, sign, scale, had):
    return jnp.clip(turn(values * sign, had) * scale, -448.0, 448.0).astype(jnp.bfloat16)


def decode(codes, scale, had):
    return jnp.dot(codes, had, preferred_element_type=jnp.float32) * scale


def project_body(a_ref, w_ref, sign_ref, scale_ref, had_ref, o_ref):
    product = jnp.dot(a_ref[...], w_ref[...], preferred_element_type=jnp.float32)
    for low in range(0, product.shape[1], 128):
        cols = slice(low, low + 128)
        o_ref[:, cols] = encode(product[:, cols], sign_ref[:, cols], scale_ref[:, cols], had_ref[...])


def project(a, w, sign, scale, had):
    rows, depth = a.shape
    width = w.shape[1]
    block = 256
    return pl.pallas_call(
        project_body,
        grid=(width // block,),
        in_specs=[
            pl.BlockSpec((rows, depth), lambda j: (0, 0)),
            pl.BlockSpec((depth, block), lambda j: (0, j)),
            pl.BlockSpec((1, block), lambda j: (0, j)),
            pl.BlockSpec((1, block), lambda j: (0, j)),
            pl.BlockSpec((128, 128), lambda j: (0, 0)),
        ],
        out_specs=pl.BlockSpec((rows, block), lambda j: (0, j)),
        out_shape=jax.ShapeDtypeStruct((rows, width), jnp.bfloat16),
        compiler_params=pltpu.CompilerParams(vmem_limit_bytes=VMEM_LIMIT),
    )(a, w, sign, scale, had)


def exchange_body(nx, parts, keep, code_ref, base_ref, dec_ref, sign_ref, scale_ref, had_ref, *refs):
    if keep:
        state_ref, *refs = refs
    (o_ref, s_ref, q_ref, g_ref, pair_send, pair_recv, sum_send, sum_recv, out_send, out_recv, fwd_send, fwd_recv) = refs
    t = lax.axis_index("tensor")
    core = lax.rem(t, 2)
    chip = t // 2
    width = code_ref.shape[3] // parts
    sibling = chip * 2 + 1 - core

    def chip_at(k):
        return lax.rem(chip + k + nx, nx)

    def span(j):
        return slice(j * width, (j + 1) * width)

    def cols(j):
        return pl.ds(j * width, width)

    def pair_copy(j):
        return pltpu.make_async_remote_copy(
            src_ref=code_ref.at[:, 1 - core, :, cols(j)], dst_ref=s_ref.at[:, :, cols(j)],
            send_sem=pair_send.at[j], recv_sem=pair_recv.at[j],
            device_id={"tensor": sibling}, device_id_type=MESH)

    def sum_copy(k, j):
        return pltpu.make_async_remote_copy(
            src_ref=q_ref.at[chip_at(k), :, cols(j)], dst_ref=g_ref.at[k - 1, :, cols(j)],
            send_sem=sum_send.at[k - 1, j], recv_sem=sum_recv.at[k - 1, j],
            device_id={"tensor": chip_at(k) * 2 + core}, device_id_type=MESH)

    def out_copy(k, j):
        part = o_ref.at[chip, core, :, cols(j)]
        return pltpu.make_async_remote_copy(
            src_ref=part, dst_ref=part, send_sem=out_send.at[k - 1, j], recv_sem=out_recv.at[k - 1, j],
            device_id={"tensor": chip_at(k) * 2 + core}, device_id_type=MESH)

    def forward_copy(k, j):
        part = o_ref.at[chip_at(-k), core, :, cols(j)]
        return pltpu.make_async_remote_copy(
            src_ref=part, dst_ref=part, send_sem=fwd_send.at[k, j], recv_sem=fwd_recv.at[k, j],
            device_id={"tensor": sibling}, device_id_type=MESH)

    barrier = pltpu.get_barrier_semaphore()
    pl.semaphore_signal(barrier, inc=1, device_id={"tensor": sibling}, device_id_type=MESH)
    for k in range(1, nx):
        pl.semaphore_signal(barrier, inc=1, device_id={"tensor": chip_at(k) * 2 + core}, device_id_type=MESH)
    pl.semaphore_wait(barrier, nx)

    for j in range(parts):
        pair_copy(j).start()
    for j in range(parts):
        pair_copy(j).wait_recv()
        for chip_to in range(nx):
            both = code_ref[chip_to, core, :, span(j)].astype(jnp.float32) + s_ref[chip_to, :, span(j)].astype(jnp.float32)
            q_ref[chip_to, :, span(j)] = both.astype(jnp.bfloat16)
        for k in range(1, nx):
            sum_copy(k, j).start()
    for j in range(parts):
        total = q_ref[chip, :, span(j)].astype(jnp.float32)
        for k in range(1, nx):
            sum_copy(k, j).wait_recv()
            total += g_ref[k - 1, :, span(j)].astype(jnp.float32)
        total = total.astype(jnp.bfloat16)
        for low in range(0, width, 128):
            here = slice(j * width + low, j * width + low + 128)
            state = base_ref[:, here].astype(jnp.float32) + decode(total[:, low:low + 128], dec_ref[:, here], had_ref[...])
            if keep:
                state_ref[:, here] = state
            o_ref[chip, core, :, here] = encode(state, sign_ref[:, here], scale_ref[:, here], had_ref[...])
        for k in range(1, nx):
            out_copy(k, j).start()
        forward_copy(0, j).start()
    for j in range(parts):
        for k in range(1, nx):
            out_copy(k, j).wait_recv()
            forward_copy(k, j).start()
    for j in range(parts):
        pair_copy(j).wait_send()
        for k in range(nx):
            forward_copy(k, j).wait()
        for k in range(1, nx):
            sum_copy(k, j).wait_send()
            out_copy(k, j).wait_send()


def exchange(n_tensor, keep, name, code, base, dec, sign, scale, had):
    rows, width = code.shape
    nx, own, parts = n_tensor // 2, rows // n_tensor, 4
    vmem = pl.BlockSpec(memory_space=pltpu.VMEM)
    states = [jax.ShapeDtypeStruct((own, width), jnp.float32)] if keep else []
    *state, out = pl.pallas_call(
        functools.partial(exchange_body, nx, parts, keep),
        out_shape=states + [jax.ShapeDtypeStruct((nx, 2, own, width), jnp.bfloat16)],
        in_specs=[vmem] * 6,
        out_specs=[vmem] * (len(states) + 1),
        scratch_shapes=[
            pltpu.VMEM((nx, own, width), jnp.bfloat16),
            pltpu.VMEM((nx, own, width), jnp.bfloat16),
            pltpu.VMEM((nx - 1, own, width), jnp.bfloat16),
            pltpu.SemaphoreType.DMA((parts,)),
            pltpu.SemaphoreType.DMA((parts,)),
            pltpu.SemaphoreType.DMA((nx - 1, parts)),
            pltpu.SemaphoreType.DMA((nx - 1, parts)),
            pltpu.SemaphoreType.DMA((nx - 1, parts)),
            pltpu.SemaphoreType.DMA((nx - 1, parts)),
            pltpu.SemaphoreType.DMA((nx, parts)),
            pltpu.SemaphoreType.DMA((nx, parts)),
        ],
        compiler_params=pltpu.CompilerParams(collective_id=name, has_side_effects=True, vmem_limit_bytes=VMEM_LIMIT),
    )(code.reshape(nx, 2, own, width), base, dec, sign, scale, had)
    return (*state, out.reshape(rows, width))


def finish_body(code_ref, dec_ref, had_ref, o_ref):
    for low in range(0, code_ref.shape[1], 128):
        cols = slice(low, low + 128)
        o_ref[:, cols] = decode(code_ref[:, cols], dec_ref[:, cols], had_ref[...]).astype(jnp.bfloat16)


def finish(code, dec, had):
    rows, width = code.shape
    block = min(width, 512)
    return pl.pallas_call(
        finish_body,
        grid=(width // block,),
        in_specs=[
            pl.BlockSpec((rows, block), lambda j: (0, j)),
            pl.BlockSpec((1, block), lambda j: (0, j)),
            pl.BlockSpec((128, 128), lambda j: (0, 0)),
        ],
        out_specs=pl.BlockSpec((rows, block), lambda j: (0, j)),
        out_shape=jax.ShapeDtypeStruct((rows, width), jnp.bfloat16),
        compiler_params=pltpu.CompilerParams(vmem_limit_bytes=VMEM_LIMIT),
    )(code, dec, had)


def ffn_body(n, chunks, cw, code_ref, dec_ref, gain_ref, had_ref, gate_ref, up_ref, h_ref,
             x_ref, sq_ref, sqr_ref, w_ref, p_ref, r_ref,
             w_sem, rs_send, rs_recv, ag_send, ag_recv, sq_send, sq_recv):
    z = lax.axis_index("request")
    half = p_ref.shape[2]

    def weights(c, slot):
        cols = pl.ds(pl.multiple_of(c * cw, cw), cw)
        return (
            pltpu.make_async_copy(gate_ref.at[:, cols], w_ref.at[slot, :, pl.ds(0, cw)], w_sem.at[slot, 0]),
            pltpu.make_async_copy(up_ref.at[:, cols], w_ref.at[slot, :, pl.ds(cw, cw)], w_sem.at[slot, 1]),
        )

    barrier = pltpu.get_barrier_semaphore()

    @pl.when(z > 0)
    def _():
        pl.semaphore_signal(barrier, inc=1, device_id={"request": z - 1}, device_id_type=MESH)

    @pl.when(z < n - 1)
    def _():
        pl.semaphore_signal(barrier, inc=1, device_id={"request": z + 1}, device_id_type=MESH)

    for copy in weights(0, 0):
        copy.start()

    sq_ref[...] = jnp.zeros_like(sq_ref)

    @pl.loop(0, code_ref.shape[1] // 128)
    def _(b):
        cols = pl.ds(pl.multiple_of(b * 128, 128), 128)
        restored = decode(code_ref[:, cols], dec_ref[:, cols], had_ref[...])
        squared = restored * restored
        sq_ref[0] += squared[:half]
        sq_ref[1] += squared[half:]
        x_ref[:, cols] = (restored * gain_ref[:, cols]).astype(jnp.bfloat16)

    pl.semaphore_wait(barrier, (z > 0).astype(jnp.int32) + (z < n - 1).astype(jnp.int32))

    place = (n - 1 - z, z)
    after = (z - 1, z + 1)
    before = (z + 1, z - 1)

    def sum_copy(d, c):
        return pltpu.make_async_remote_copy(
            src_ref=p_ref.at[d, c], dst_ref=r_ref.at[d, c], send_sem=rs_send.at[d, c], recv_sem=rs_recv.at[d, c],
            device_id={"request": after[d]}, device_id_type=MESH)

    def square_copy(d):
        return pltpu.make_async_remote_copy(
            src_ref=sq_ref.at[d], dst_ref=sqr_ref.at[d], send_sem=sq_send.at[d], recv_sem=sq_recv.at[d],
            device_id={"request": after[d]}, device_id_type=MESH)

    def hidden_copy(d, c):
        part = h_ref.at[pl.ds(d * half, half), pl.ds(pl.multiple_of(c * cw, cw), cw)]
        return pltpu.make_async_remote_copy(
            src_ref=part, dst_ref=part, send_sem=ag_send.at[d, c], recv_sem=ag_recv.at[d, c],
            device_id={"request": before[d]}, device_id_type=MESH)

    @pl.loop(0, chunks + 2 * (n - 1) * LAG)
    def _(s):
        @pl.when(s < chunks)
        def _():
            slot = lax.rem(s, 2)

            @pl.when(s + 1 < chunks)
            def _():
                for copy in weights(s + 1, 1 - slot):
                    copy.start()

            for copy in weights(s, slot):
                copy.wait()
            total = jnp.dot(x_ref[...], w_ref[slot], preferred_element_type=jnp.float32).astype(jnp.bfloat16)
            p_ref[0, s] = total[:half]
            p_ref[1, s] = total[half:]

        for d in (0, 1):
            pos = place[d]
            c = s - pos * LAG

            @pl.when((c >= 0) & (c < chunks))
            def _(d=d, pos=pos, c=c):
                @pl.when(c == 0)
                def _():
                    @pl.when(pos > 0)
                    def _():
                        square_copy(d).wait_recv()
                        sq_ref[d] += sqr_ref[d]

                    @pl.when(pos < n - 1)
                    def _():
                        square_copy(d).start()

                    @pl.when(pos == n - 1)
                    def _():
                        total = jnp.sum(sq_ref[d], axis=1, keepdims=True)
                        sq_ref[d] = jnp.broadcast_to(lax.rsqrt(total / D + 1e-05), sq_ref.shape[1:])

                @pl.when(pos > 0)
                def _():
                    sum_copy(d, c).wait_recv()
                    p_ref[d, c] = (p_ref[d, c].astype(jnp.float32) + r_ref[d, c].astype(jnp.float32)).astype(jnp.bfloat16)

                @pl.when(pos < n - 1)
                def _():
                    sum_copy(d, c).start()

                @pl.when(pos == n - 1)
                def _():
                    cols = pl.multiple_of(c * cw, cw)
                    for low in range(0, cw, 128):
                        factor = sq_ref[d]
                        gate = p_ref[d, c, :, low:low + 128].astype(jnp.float32) * factor
                        up = p_ref[d, c, :, cw + low:cw + low + 128].astype(jnp.float32) * factor
                        value = gate / (1.0 + jnp.exp(-gate)) * up
                        h_ref[pl.ds(d * half, half), pl.ds(pl.multiple_of(cols + low, 128), 128)] = value.astype(jnp.bfloat16)
                    hidden_copy(d, c).start()

            back = s - (2 * (n - 1) - pos) * LAG

            @pl.when((pos < n - 1) & (back >= 0) & (back < chunks))
            def _(d=d, pos=pos, back=back):
                hidden_copy(d, back).wait_recv()

                @pl.when(pos > 0)
                def _():
                    hidden_copy(d, back).start()

    for d in (0, 1):
        pos = place[d]

        @pl.when(pos < n - 1)
        def _(d=d):
            square_copy(d).wait_send()

            @pl.loop(0, chunks)
            def _(c):
                sum_copy(d, c).wait_send()

        @pl.when(pos > 0)
        def _(d=d):
            @pl.loop(0, chunks)
            def _(c):
                hidden_copy(d, c).wait_send()


def ffn(n, code, dec, gain, had, gate_weight, up_weight):
    rows, depth = code.shape
    units = gate_weight.shape[1]
    cw = 128
    chunks = units // cw
    half = rows // 2
    vmem = pl.BlockSpec(memory_space=pltpu.VMEM)
    return pl.pallas_call(
        functools.partial(ffn_body, n, chunks, cw),
        out_shape=jax.ShapeDtypeStruct((rows, units), jnp.bfloat16),
        in_specs=[vmem] * 4 + [pl.BlockSpec(memory_space=pl.ANY)] * 2,
        out_specs=vmem,
        scratch_shapes=[
            pltpu.VMEM((rows, depth), jnp.bfloat16),
            pltpu.VMEM((2, half, 128), jnp.float32),
            pltpu.VMEM((2, half, 128), jnp.float32),
            pltpu.VMEM((2, depth, 2 * cw), jnp.bfloat16),
            pltpu.VMEM((2, chunks, half, 2 * cw), jnp.bfloat16),
            pltpu.VMEM((2, chunks, half, 2 * cw), jnp.bfloat16),
            pltpu.SemaphoreType.DMA((2, 2)),
            pltpu.SemaphoreType.DMA((2, chunks)),
            pltpu.SemaphoreType.DMA((2, chunks)),
            pltpu.SemaphoreType.DMA((2, chunks)),
            pltpu.SemaphoreType.DMA((2, chunks)),
            pltpu.SemaphoreType.DMA((2,)),
            pltpu.SemaphoreType.DMA((2,)),
        ],
        compiler_params=pltpu.CompilerParams(collective_id=0, has_side_effects=True, vmem_limit_bytes=VMEM_LIMIT),
    )(code, dec, gain, had, gate_weight, up_weight)


def shards(n_tensor, n_request, attn_heads, out_weight, resid, gain, gate_weight, up_weight, down_weight, signs, expos):
    had = hadamard()
    sign = (2 * signs - 1).astype(jnp.float32)
    shift = expos + jnp.array([[4], [8], [4], [6]], jnp.int32)
    enc = jnp.repeat(0.125 * jnp.exp2(-shift.astype(jnp.float32)), 128, axis=1)
    dec = jnp.repeat(0.0625 * jnp.exp2(shift.astype(jnp.float32)), 128, axis=1) * sign
    row = lambda table, k: table[k:k + 1]

    coded = project(attn_heads, out_weight, row(sign, 0), row(enc, 0), had)
    hidden_state, gathered = exchange(n_tensor, True, 1, coded, resid, row(dec, 0), row(sign, 1), row(enc, 1), had)
    hidden = ffn(n_request, gathered, row(dec, 1), gain.astype(jnp.float32)[None, :], had, gate_weight, up_weight)
    coded = project(hidden, down_weight, row(sign, 2), row(enc, 2), had)
    (gathered,) = exchange(n_tensor, False, 2, coded, hidden_state, row(dec, 2), row(sign, 3), row(enc, 3), had)
    return finish(gathered, row(dec, 3), had)


def solution(mesh):
    return jax.shard_map(
        functools.partial(shards, mesh.shape["tensor"], mesh.shape["request"]),
        mesh=mesh,
        in_specs=(
            P("parts", "tensor"),
            P("tensor", "request"),
            P(("parts", "tensor"), "request"),
            P("request"),
            P("request", "tensor"),
            P("request", "tensor"),
            P("tensor", "request"),
            P(None, "request"),
            P(None, "request"),
        ),
        out_specs=P("parts", "request"),
        check_vma=False,
    )
```

```python
import functools

import jax
import jax.numpy as jnp
from jax import lax
from jax.experimental import pallas as pl
from jax.experimental.pallas import tpu as pltpu
from jax.sharding import PartitionSpec as P

D = 8192
MESH = pl.DeviceIdType.MESH
LAG = 2
VMEM_LIMIT = 52 * 2**20


def hadamard():
    index = jnp.arange(128, dtype=jnp.int32)
    common = jnp.bitwise_and(index[:, None], index[None, :])
    ones_count = jnp.zeros((128, 128), jnp.int32)
    for level in range(7):
        ones_count = ones_count + jnp.bitwise_and(jnp.right_shift(common, level), 1)
    return (1 - 2 * (ones_count % 2)).astype(jnp.bfloat16)


def turn(values, had):
    high = values.astype(jnp.bfloat16)
    low = (values - high.astype(jnp.float32)).astype(jnp.bfloat16)
    return jnp.dot(high, had, preferred_element_type=jnp.float32) + jnp.dot(low, had, preferred_element_type=jnp.float32)


def encode(values, sign, scale, had):
    return jnp.clip(turn(values * sign, had) * scale, -448.0, 448.0).astype(jnp.bfloat16)


def decode(codes, scale, had):
    return jnp.dot(codes, had, preferred_element_type=jnp.float32) * scale


def project_body(a_ref, w_ref, sign_ref, scale_ref, had_ref, o_ref):
    product = jnp.dot(a_ref[...], w_ref[...], preferred_element_type=jnp.float32)
    for low in range(0, product.shape[1], 128):
        cols = slice(low, low + 128)
        o_ref[:, cols] = encode(product[:, cols], sign_ref[:, cols], scale_ref[:, cols], had_ref[...])


def project(a, w, sign, scale, had):
    rows, depth = a.shape
    width = w.shape[1]
    block = 256
    return pl.pallas_call(
        project_body,
        grid=(width // block,),
        in_specs=[
            pl.BlockSpec((rows, depth), lambda j: (0, 0)),
            pl.BlockSpec((depth, block), lambda j: (0, j)),
            pl.BlockSpec((1, block), lambda j: (0, j)),
            pl.BlockSpec((1, block), lambda j: (0, j)),
            pl.BlockSpec((128, 128), lambda j: (0, 0)),
        ],
        out_specs=pl.BlockSpec((rows, block), lambda j: (0, j)),
        out_shape=jax.ShapeDtypeStruct((rows, width), jnp.bfloat16),
        compiler_params=pltpu.CompilerParams(vmem_limit_bytes=VMEM_LIMIT),
    )(a, w, sign, scale, had)


def exchange_body(nx, parts, keep, code_ref, base_ref, dec_ref, sign_ref, scale_ref, had_ref, *refs):
    if keep:
        state_ref, *refs = refs
    (o_ref, s_ref, q_ref, g_ref, pair_send, pair_recv, sum_send, sum_recv, out_send, out_recv, fwd_send, fwd_recv) = refs
    t = lax.axis_index("tensor")
    core = lax.rem(t, 2)
    chip = t // 2
    width = code_ref.shape[3] // parts
    sibling = chip * 2 + 1 - core

    def chip_at(k):
        return lax.rem(chip + k + nx, nx)

    def span(j):
        return slice(j * width, (j + 1) * width)

    def cols(j):
        return pl.ds(j * width, width)

    def pair_copy(j):
        return pltpu.make_async_remote_copy(
            src_ref=code_ref.at[:, 1 - core, :, cols(j)], dst_ref=s_ref.at[:, :, cols(j)],
            send_sem=pair_send.at[j], recv_sem=pair_recv.at[j],
            device_id={"tensor": sibling}, device_id_type=MESH)

    def sum_copy(k, j):
        return pltpu.make_async_remote_copy(
            src_ref=q_ref.at[chip_at(k), :, cols(j)], dst_ref=g_ref.at[k - 1, :, cols(j)],
            send_sem=sum_send.at[k - 1, j], recv_sem=sum_recv.at[k - 1, j],
            device_id={"tensor": chip_at(k) * 2 + core}, device_id_type=MESH)

    def out_copy(k, j):
        part = o_ref.at[chip, core, :, cols(j)]
        return pltpu.make_async_remote_copy(
            src_ref=part, dst_ref=part, send_sem=out_send.at[k - 1, j], recv_sem=out_recv.at[k - 1, j],
            device_id={"tensor": chip_at(k) * 2 + core}, device_id_type=MESH)

    def forward_copy(k, j):
        part = o_ref.at[chip_at(-k), core, :, cols(j)]
        return pltpu.make_async_remote_copy(
            src_ref=part, dst_ref=part, send_sem=fwd_send.at[k, j], recv_sem=fwd_recv.at[k, j],
            device_id={"tensor": sibling}, device_id_type=MESH)

    barrier = pltpu.get_barrier_semaphore()
    pl.semaphore_signal(barrier, inc=1, device_id={"tensor": sibling}, device_id_type=MESH)
    for k in range(1, nx):
        pl.semaphore_signal(barrier, inc=1, device_id={"tensor": chip_at(k) * 2 + core}, device_id_type=MESH)
    pl.semaphore_wait(barrier, nx)

    for j in range(parts):
        pair_copy(j).start()
    for j in range(parts):
        pair_copy(j).wait_recv()
        for chip_to in range(nx):
            both = code_ref[chip_to, core, :, span(j)].astype(jnp.float32) + s_ref[chip_to, :, span(j)].astype(jnp.float32)
            q_ref[chip_to, :, span(j)] = both.astype(jnp.bfloat16)
        for k in range(1, nx):
            sum_copy(k, j).start()
    for j in range(parts):
        total = q_ref[chip, :, span(j)].astype(jnp.float32)
        for k in range(1, nx):
            sum_copy(k, j).wait_recv()
            total += g_ref[k - 1, :, span(j)].astype(jnp.float32)
        total = total.astype(jnp.bfloat16)
        for low in range(0, width, 128):
            here = slice(j * width + low, j * width + low + 128)
            state = base_ref[:, here].astype(jnp.float32) + decode(total[:, low:low + 128], dec_ref[:, here], had_ref[...])
            if keep:
                state_ref[:, here] = state
            o_ref[chip, core, :, here] = encode(state, sign_ref[:, here], scale_ref[:, here], had_ref[...])
        for k in range(1, nx):
            out_copy(k, j).start()
        forward_copy(0, j).start()
    for j in range(parts):
        for k in range(1, nx):
            out_copy(k, j).wait_recv()
            forward_copy(k, j).start()
    for j in range(parts):
        pair_copy(j).wait_send()
        for k in range(nx):
            forward_copy(k, j).wait()
        for k in range(1, nx):
            sum_copy(k, j).wait_send()
            out_copy(k, j).wait_send()


def exchange(n_tensor, keep, name, code, base, dec, sign, scale, had):
    rows, width = code.shape
    nx, own, parts = n_tensor // 2, rows // n_tensor, 4
    vmem = pl.BlockSpec(memory_space=pltpu.VMEM)
    states = [jax.ShapeDtypeStruct((own, width), jnp.float32)] if keep else []
    *state, out = pl.pallas_call(
        functools.partial(exchange_body, nx, parts, keep),
        out_shape=states + [jax.ShapeDtypeStruct((nx, 2, own, width), jnp.bfloat16)],
        in_specs=[vmem] * 6,
        out_specs=[vmem] * (len(states) + 1),
        scratch_shapes=[
            pltpu.VMEM((nx, own, width), jnp.bfloat16),
            pltpu.VMEM((nx, own, width), jnp.bfloat16),
            pltpu.VMEM((nx - 1, own, width), jnp.bfloat16),
            pltpu.SemaphoreType.DMA((parts,)),
            pltpu.SemaphoreType.DMA((parts,)),
            pltpu.SemaphoreType.DMA((nx - 1, parts)),
            pltpu.SemaphoreType.DMA((nx - 1, parts)),
            pltpu.SemaphoreType.DMA((nx - 1, parts)),
            pltpu.SemaphoreType.DMA((nx - 1, parts)),
            pltpu.SemaphoreType.DMA((nx, parts)),
            pltpu.SemaphoreType.DMA((nx, parts)),
        ],
        compiler_params=pltpu.CompilerParams(collective_id=name, has_side_effects=True, vmem_limit_bytes=VMEM_LIMIT),
    )(code.reshape(nx, 2, own, width), base, dec, sign, scale, had)
    return (*state, out.reshape(rows, width))


def finish_body(code_ref, dec_ref, had_ref, o_ref):
    for low in range(0, code_ref.shape[1], 128):
        cols = slice(low, low + 128)
        o_ref[:, cols] = decode(code_ref[:, cols], dec_ref[:, cols], had_ref[...]).astype(jnp.bfloat16)


def finish(code, dec, had):
    rows, width = code.shape
    block = min(width, 512)
    return pl.pallas_call(
        finish_body,
        grid=(width // block,),
        in_specs=[
            pl.BlockSpec((rows, block), lambda j: (0, j)),
            pl.BlockSpec((1, block), lambda j: (0, j)),
            pl.BlockSpec((128, 128), lambda j: (0, 0)),
        ],
        out_specs=pl.BlockSpec((rows, block), lambda j: (0, j)),
        out_shape=jax.ShapeDtypeStruct((rows, width), jnp.bfloat16),
        compiler_params=pltpu.CompilerParams(vmem_limit_bytes=VMEM_LIMIT),
    )(code, dec, had)


def ffn_body(n, chunks, cw, code_ref, dec_ref, gain_ref, had_ref, sign_ref, scale_ref, gate_ref, up_ref, down_ref, o_ref,
             h_ref, down_held, acc_ref, down_sem, x_ref, sq_ref, sqr_ref, w_ref, p_ref, r_ref,
             w_sem, rs_send, rs_recv, ag_send, ag_recv, sq_send, sq_recv):
    z = lax.axis_index("request")
    half = p_ref.shape[2]

    def weights(c, slot):
        cols = pl.ds(pl.multiple_of(c * cw, cw), cw)
        return (
            pltpu.make_async_copy(gate_ref.at[:, cols], w_ref.at[slot, :, pl.ds(0, cw)], w_sem.at[slot, 0]),
            pltpu.make_async_copy(up_ref.at[:, cols], w_ref.at[slot, :, pl.ds(cw, cw)], w_sem.at[slot, 1]),
        )

    barrier = pltpu.get_barrier_semaphore()

    @pl.when(z > 0)
    def _():
        pl.semaphore_signal(barrier, inc=1, device_id={"request": z - 1}, device_id_type=MESH)

    @pl.when(z < n - 1)
    def _():
        pl.semaphore_signal(barrier, inc=1, device_id={"request": z + 1}, device_id_type=MESH)

    for copy in weights(0, 0):
        copy.start()

    down_copy = pltpu.make_async_copy(down_ref, down_held, down_sem)
    down_copy.start()
    sq_ref[...] = jnp.zeros_like(sq_ref)
    acc_ref[...] = jnp.zeros_like(acc_ref)
    group = 2 if chunks % 2 == 0 else 1
    tile = min(512, acc_ref.shape[2])

    @pl.loop(0, code_ref.shape[1] // 128)
    def _(b):
        cols = pl.ds(pl.multiple_of(b * 128, 128), 128)
        restored = decode(code_ref[:, cols], dec_ref[:, cols], had_ref[...])
        squared = restored * restored
        sq_ref[0] += squared[:half]
        sq_ref[1] += squared[half:]
        x_ref[:, cols] = (restored * gain_ref[:, cols]).astype(jnp.bfloat16)

    pl.semaphore_wait(barrier, (z > 0).astype(jnp.int32) + (z < n - 1).astype(jnp.int32))

    place = (n - 1 - z, z)
    after = (z - 1, z + 1)
    before = (z + 1, z - 1)

    def sum_copy(d, c):
        return pltpu.make_async_remote_copy(
            src_ref=p_ref.at[d, c], dst_ref=r_ref.at[d, c], send_sem=rs_send.at[d, c], recv_sem=rs_recv.at[d, c],
            device_id={"request": after[d]}, device_id_type=MESH)

    def square_copy(d):
        return pltpu.make_async_remote_copy(
            src_ref=sq_ref.at[d], dst_ref=sqr_ref.at[d], send_sem=sq_send.at[d], recv_sem=sq_recv.at[d],
            device_id={"request": after[d]}, device_id_type=MESH)

    def hidden_copy(d, c):
        part = h_ref.at[pl.ds(d * half, half), pl.ds(pl.multiple_of(c * cw, cw), cw)]
        return pltpu.make_async_remote_copy(
            src_ref=part, dst_ref=part, send_sem=ag_send.at[d, c], recv_sem=ag_recv.at[d, c],
            device_id={"request": before[d]}, device_id_type=MESH)

    @pl.loop(0, chunks + 2 * (n - 1) * LAG)
    def _(s):
        @pl.when(s < chunks)
        def _():
            slot = lax.rem(s, 2)

            @pl.when(s + 1 < chunks)
            def _():
                for copy in weights(s + 1, 1 - slot):
                    copy.start()

            for copy in weights(s, slot):
                copy.wait()
            total = jnp.dot(x_ref[...], w_ref[slot], preferred_element_type=jnp.float32).astype(jnp.bfloat16)
            p_ref[0, s] = total[:half]
            p_ref[1, s] = total[half:]

        for d in (0, 1):
            pos = place[d]
            c = s - pos * LAG

            @pl.when((c >= 0) & (c < chunks))
            def _(d=d, pos=pos, c=c):
                @pl.when(c == 0)
                def _():
                    @pl.when(pos > 0)
                    def _():
                        square_copy(d).wait_recv()
                        sq_ref[d] += sqr_ref[d]

                    @pl.when(pos < n - 1)
                    def _():
                        square_copy(d).start()

                    @pl.when(pos == n - 1)
                    def _():
                        total = jnp.sum(sq_ref[d], axis=1, keepdims=True)
                        sq_ref[d] = jnp.broadcast_to(lax.rsqrt(total / D + 1e-05), sq_ref.shape[1:])

                @pl.when(pos > 0)
                def _():
                    sum_copy(d, c).wait_recv()
                    p_ref[d, c] = (p_ref[d, c].astype(jnp.float32) + r_ref[d, c].astype(jnp.float32)).astype(jnp.bfloat16)

                @pl.when(pos < n - 1)
                def _():
                    sum_copy(d, c).start()

                @pl.when(pos == n - 1)
                def _():
                    cols = pl.multiple_of(c * cw, cw)
                    for low in range(0, cw, 128):
                        factor = sq_ref[d]
                        gate = p_ref[d, c, :, low:low + 128].astype(jnp.float32) * factor
                        up = p_ref[d, c, :, cw + low:cw + low + 128].astype(jnp.float32) * factor
                        value = gate / (1.0 + jnp.exp(-gate)) * up
                        h_ref[pl.ds(d * half, half), pl.ds(pl.multiple_of(cols + low, 128), 128)] = value.astype(jnp.bfloat16)
                    hidden_copy(d, c).start()

            back = s - (2 * (n - 1) - pos) * LAG

            @pl.when((pos < n - 1) & (back >= 0) & (back < chunks))
            def _(d=d, pos=pos, back=back):
                hidden_copy(d, back).wait_recv()

                @pl.when(pos > 0)
                def _():
                    hidden_copy(d, back).start()

        @pl.when(s == (n - 1) * LAG)
        def _():
            down_copy.wait()

        for d in (0, 1):
            back = s - (2 * (n - 1) - place[d]) * LAG

            @pl.when((back >= 0) & (back < chunks) & (lax.rem(back, group) == group - 1))
            def _(d=d, back=back):
                units = pl.ds(pl.multiple_of((back - (group - 1)) * cw, cw), group * cw)
                part = h_ref[pl.ds(d * half, half), units]

                @pl.loop(0, acc_ref.shape[2] // tile)
                def _(i):
                    cols = pl.ds(pl.multiple_of(i * tile, tile), tile)
                    acc_ref[d, :, cols] += jnp.dot(part, down_held[units, cols], preferred_element_type=jnp.float32)

    @pl.loop(0, acc_ref.shape[2] // 128)
    def _(b):
        cols = pl.ds(pl.multiple_of(b * 128, 128), 128)
        for d in (0, 1):
            o_ref[pl.ds(d * half, half), cols] = encode(acc_ref[d, :, cols], sign_ref[:, cols], scale_ref[:, cols], had_ref[...])

    for d in (0, 1):
        pos = place[d]

        @pl.when(pos < n - 1)
        def _(d=d):
            square_copy(d).wait_send()

            @pl.loop(0, chunks)
            def _(c):
                sum_copy(d, c).wait_send()

        @pl.when(pos > 0)
        def _(d=d):
            @pl.loop(0, chunks)
            def _(c):
                hidden_copy(d, c).wait_send()


def ffn(n, code, dec, gain, had, sign, scale, gate_weight, up_weight, down_weight):
    rows, depth = code.shape
    units = gate_weight.shape[1]
    cw = 128
    chunks = units // cw
    half = rows // 2
    vmem = pl.BlockSpec(memory_space=pltpu.VMEM)
    return pl.pallas_call(
        functools.partial(ffn_body, n, chunks, cw),
        out_shape=jax.ShapeDtypeStruct((rows, down_weight.shape[1]), jnp.bfloat16),
        in_specs=[vmem] * 6 + [pl.BlockSpec(memory_space=pl.ANY)] * 3,
        out_specs=vmem,
        scratch_shapes=[
            pltpu.VMEM((rows, units), jnp.bfloat16),
            pltpu.VMEM(down_weight.shape, jnp.bfloat16),
            pltpu.VMEM((2, half, down_weight.shape[1]), jnp.float32),
            pltpu.SemaphoreType.DMA,
            pltpu.VMEM((rows, depth), jnp.bfloat16),
            pltpu.VMEM((2, half, 128), jnp.float32),
            pltpu.VMEM((2, half, 128), jnp.float32),
            pltpu.VMEM((2, depth, 2 * cw), jnp.bfloat16),
            pltpu.VMEM((2, chunks, half, 2 * cw), jnp.bfloat16),
            pltpu.VMEM((2, chunks, half, 2 * cw), jnp.bfloat16),
            pltpu.SemaphoreType.DMA((2, 2)),
            pltpu.SemaphoreType.DMA((2, chunks)),
            pltpu.SemaphoreType.DMA((2, chunks)),
            pltpu.SemaphoreType.DMA((2, chunks)),
            pltpu.SemaphoreType.DMA((2, chunks)),
            pltpu.SemaphoreType.DMA((2,)),
            pltpu.SemaphoreType.DMA((2,)),
        ],
        compiler_params=pltpu.CompilerParams(collective_id=0, has_side_effects=True, vmem_limit_bytes=VMEM_LIMIT),
    )(code, dec, gain, had, sign, scale, gate_weight, up_weight, down_weight)


def shards(n_tensor, n_request, attn_heads, out_weight, resid, gain, gate_weight, up_weight, down_weight, signs, expos):
    had = hadamard()
    sign = (2 * signs - 1).astype(jnp.float32)
    shift = expos + jnp.array([[4], [8], [4], [6]], jnp.int32)
    enc = jnp.repeat(0.125 * jnp.exp2(-shift.astype(jnp.float32)), 128, axis=1)
    dec = jnp.repeat(0.0625 * jnp.exp2(shift.astype(jnp.float32)), 128, axis=1) * sign
    row = lambda table, k: table[k:k + 1]

    coded = project(attn_heads, out_weight, row(sign, 0), row(enc, 0), had)
    hidden_state, gathered = exchange(n_tensor, True, 1, coded, resid, row(dec, 0), row(sign, 1), row(enc, 1), had)
    coded = ffn(
        n_request, gathered, row(dec, 1), gain.astype(jnp.float32)[None, :], had, row(sign, 2), row(enc, 2),
        gate_weight, up_weight, down_weight)
    (gathered,) = exchange(n_tensor, False, 2, coded, hidden_state, row(dec, 2), row(sign, 3), row(enc, 3), had)
    return finish(gathered, row(dec, 3), had)


def solution(mesh):
    return jax.shard_map(
        functools.partial(shards, mesh.shape["tensor"], mesh.shape["request"]),
        mesh=mesh,
        in_specs=(
            P("parts", "tensor"),
            P("tensor", "request"),
            P(("parts", "tensor"), "request"),
            P("request"),
            P("request", "tensor"),
            P("request", "tensor"),
            P("tensor", "request"),
            P(None, "request"),
            P(None, "request"),
        ),
        out_specs=P("parts", "request"),
        check_vma=False,
    )
```

```python
import functools

import jax
import jax.numpy as jnp
from jax import lax
from jax.experimental import pallas as pl
from jax.experimental.pallas import tpu as pltpu
from jax.sharding import PartitionSpec as P

D = 8192
MESH = pl.DeviceIdType.MESH
LAG = 1
VMEM_LIMIT = 52 * 2**20


def hadamard():
    index = jnp.arange(128, dtype=jnp.int32)
    common = jnp.bitwise_and(index[:, None], index[None, :])
    ones_count = jnp.zeros((128, 128), jnp.int32)
    for level in range(7):
        ones_count = ones_count + jnp.bitwise_and(jnp.right_shift(common, level), 1)
    return (1 - 2 * (ones_count % 2)).astype(jnp.bfloat16)


def turn(values, had):
    high = values.astype(jnp.bfloat16)
    low = (values - high.astype(jnp.float32)).astype(jnp.bfloat16)
    return jnp.dot(high, had, preferred_element_type=jnp.float32) + jnp.dot(low, had, preferred_element_type=jnp.float32)


def encode(values, sign, scale, had):
    return jnp.clip(turn(values * sign, had) * scale, -448.0, 448.0).astype(jnp.bfloat16)


def decode(codes, scale, had):
    return jnp.dot(codes, had, preferred_element_type=jnp.float32) * scale


def project_body(a_ref, w_ref, sign_ref, scale_ref, had_ref, o_ref):
    product = jnp.dot(a_ref[...], w_ref[...], preferred_element_type=jnp.float32)
    for low in range(0, product.shape[1], 128):
        cols = slice(low, low + 128)
        o_ref[:, cols] = encode(product[:, cols], sign_ref[:, cols], scale_ref[:, cols], had_ref[...])


def project(a, w, sign, scale, had):
    rows, depth = a.shape
    width = w.shape[1]
    block = 256
    return pl.pallas_call(
        project_body,
        grid=(width // block,),
        in_specs=[
            pl.BlockSpec((rows, depth), lambda j: (0, 0)),
            pl.BlockSpec((depth, block), lambda j: (0, j)),
            pl.BlockSpec((1, block), lambda j: (0, j)),
            pl.BlockSpec((1, block), lambda j: (0, j)),
            pl.BlockSpec((128, 128), lambda j: (0, 0)),
        ],
        out_specs=pl.BlockSpec((rows, block), lambda j: (0, j)),
        out_shape=jax.ShapeDtypeStruct((rows, width), jnp.bfloat16),
        compiler_params=pltpu.CompilerParams(vmem_limit_bytes=VMEM_LIMIT),
    )(a, w, sign, scale, had)


def exchange_body(nx, parts, keep, code_ref, base_ref, dec_ref, sign_ref, scale_ref, had_ref, *refs):
    if keep:
        state_ref, *refs = refs
    (o_ref, s_ref, q_ref, g_ref, pair_send, pair_recv, sum_send, sum_recv, out_send, out_recv, fwd_send, fwd_recv) = refs
    t = lax.axis_index("tensor")
    core = lax.rem(t, 2)
    chip = t // 2
    width = code_ref.shape[3] // parts
    sibling = chip * 2 + 1 - core

    def chip_at(k):
        return lax.rem(chip + k + nx, nx)

    def span(j):
        return slice(j * width, (j + 1) * width)

    def cols(j):
        return pl.ds(j * width, width)

    def pair_copy(j):
        return pltpu.make_async_remote_copy(
            src_ref=code_ref.at[:, 1 - core, :, cols(j)], dst_ref=s_ref.at[:, :, cols(j)],
            send_sem=pair_send.at[j], recv_sem=pair_recv.at[j],
            device_id={"tensor": sibling}, device_id_type=MESH)

    def sum_copy(k, j):
        return pltpu.make_async_remote_copy(
            src_ref=q_ref.at[chip_at(k), :, cols(j)], dst_ref=g_ref.at[k - 1, :, cols(j)],
            send_sem=sum_send.at[k - 1, j], recv_sem=sum_recv.at[k - 1, j],
            device_id={"tensor": chip_at(k) * 2 + core}, device_id_type=MESH)

    def out_copy(k, j):
        part = o_ref.at[chip, core, :, cols(j)]
        return pltpu.make_async_remote_copy(
            src_ref=part, dst_ref=part, send_sem=out_send.at[k - 1, j], recv_sem=out_recv.at[k - 1, j],
            device_id={"tensor": chip_at(k) * 2 + core}, device_id_type=MESH)

    def forward_copy(k, j):
        part = o_ref.at[chip_at(-k), core, :, cols(j)]
        return pltpu.make_async_remote_copy(
            src_ref=part, dst_ref=part, send_sem=fwd_send.at[k, j], recv_sem=fwd_recv.at[k, j],
            device_id={"tensor": sibling}, device_id_type=MESH)

    barrier = pltpu.get_barrier_semaphore()
    pl.semaphore_signal(barrier, inc=1, device_id={"tensor": sibling}, device_id_type=MESH)
    for k in range(1, nx):
        pl.semaphore_signal(barrier, inc=1, device_id={"tensor": chip_at(k) * 2 + core}, device_id_type=MESH)
    pl.semaphore_wait(barrier, nx)

    for j in range(parts):
        pair_copy(j).start()
    for j in range(parts):
        pair_copy(j).wait_recv()
        for chip_to in range(nx):
            both = code_ref[chip_to, core, :, span(j)].astype(jnp.float32) + s_ref[chip_to, :, span(j)].astype(jnp.float32)
            q_ref[chip_to, :, span(j)] = both.astype(jnp.bfloat16)
        for k in range(1, nx):
            sum_copy(k, j).start()
    for j in range(parts):
        total = q_ref[chip, :, span(j)].astype(jnp.float32)
        for k in range(1, nx):
            sum_copy(k, j).wait_recv()
            total += g_ref[k - 1, :, span(j)].astype(jnp.float32)
        total = total.astype(jnp.bfloat16)
        for low in range(0, width, 128):
            here = slice(j * width + low, j * width + low + 128)
            state = base_ref[:, here].astype(jnp.float32) + decode(total[:, low:low + 128], dec_ref[:, here], had_ref[...])
            if keep:
                state_ref[:, here] = state
            o_ref[chip, core, :, here] = encode(state, sign_ref[:, here], scale_ref[:, here], had_ref[...])
        for k in range(1, nx):
            out_copy(k, j).start()
        forward_copy(0, j).start()
    for j in range(parts):
        for k in range(1, nx):
            out_copy(k, j).wait_recv()
            forward_copy(k, j).start()
    for j in range(parts):
        pair_copy(j).wait_send()
        for k in range(nx):
            forward_copy(k, j).wait()
        for k in range(1, nx):
            sum_copy(k, j).wait_send()
            out_copy(k, j).wait_send()


def exchange(n_tensor, keep, name, code, base, dec, sign, scale, had):
    rows, width = code.shape
    nx, own, parts = n_tensor // 2, rows // n_tensor, 4
    vmem = pl.BlockSpec(memory_space=pltpu.VMEM)
    states = [jax.ShapeDtypeStruct((own, width), jnp.float32)] if keep else []
    *state, out = pl.pallas_call(
        functools.partial(exchange_body, nx, parts, keep),
        out_shape=states + [jax.ShapeDtypeStruct((nx, 2, own, width), jnp.bfloat16)],
        in_specs=[vmem] * 6,
        out_specs=[vmem] * (len(states) + 1),
        scratch_shapes=[
            pltpu.VMEM((nx, own, width), jnp.bfloat16),
            pltpu.VMEM((nx, own, width), jnp.bfloat16),
            pltpu.VMEM((nx - 1, own, width), jnp.bfloat16),
            pltpu.SemaphoreType.DMA((parts,)),
            pltpu.SemaphoreType.DMA((parts,)),
            pltpu.SemaphoreType.DMA((nx - 1, parts)),
            pltpu.SemaphoreType.DMA((nx - 1, parts)),
            pltpu.SemaphoreType.DMA((nx - 1, parts)),
            pltpu.SemaphoreType.DMA((nx - 1, parts)),
            pltpu.SemaphoreType.DMA((nx, parts)),
            pltpu.SemaphoreType.DMA((nx, parts)),
        ],
        compiler_params=pltpu.CompilerParams(collective_id=name, has_side_effects=True, vmem_limit_bytes=VMEM_LIMIT),
    )(code.reshape(nx, 2, own, width), base, dec, sign, scale, had)
    return (*state, out.reshape(rows, width))


def finish_body(code_ref, dec_ref, had_ref, o_ref):
    for low in range(0, code_ref.shape[1], 128):
        cols = slice(low, low + 128)
        o_ref[:, cols] = decode(code_ref[:, cols], dec_ref[:, cols], had_ref[...]).astype(jnp.bfloat16)


def finish(code, dec, had):
    rows, width = code.shape
    block = min(width, 512)
    return pl.pallas_call(
        finish_body,
        grid=(width // block,),
        in_specs=[
            pl.BlockSpec((rows, block), lambda j: (0, j)),
            pl.BlockSpec((1, block), lambda j: (0, j)),
            pl.BlockSpec((128, 128), lambda j: (0, 0)),
        ],
        out_specs=pl.BlockSpec((rows, block), lambda j: (0, j)),
        out_shape=jax.ShapeDtypeStruct((rows, width), jnp.bfloat16),
        compiler_params=pltpu.CompilerParams(vmem_limit_bytes=VMEM_LIMIT),
    )(code, dec, had)


def ffn_body(n, chunks, cw, code_ref, dec_ref, gain_ref, had_ref, sign_ref, scale_ref, gate_ref, up_ref, down_ref, o_ref,
             h_ref, down_held, acc_ref, down_sem, x_ref, sq_ref, sqr_ref, w_ref, p_ref, r_ref,
             w_sem, rs_send, rs_recv, ag_send, ag_recv, sq_send, sq_recv):
    z = lax.axis_index("request")
    half = p_ref.shape[2]

    def weights(c, slot):
        cols = pl.ds(pl.multiple_of(c * cw, cw), cw)
        return (
            pltpu.make_async_copy(gate_ref.at[:, cols], w_ref.at[slot, :, pl.ds(0, cw)], w_sem.at[slot, 0]),
            pltpu.make_async_copy(up_ref.at[:, cols], w_ref.at[slot, :, pl.ds(cw, cw)], w_sem.at[slot, 1]),
        )

    barrier = pltpu.get_barrier_semaphore()

    @pl.when(z > 0)
    def _():
        pl.semaphore_signal(barrier, inc=1, device_id={"request": z - 1}, device_id_type=MESH)

    @pl.when(z < n - 1)
    def _():
        pl.semaphore_signal(barrier, inc=1, device_id={"request": z + 1}, device_id_type=MESH)

    for copy in weights(0, 0):
        copy.start()

    down_copy = pltpu.make_async_copy(down_ref, down_held, down_sem)
    down_copy.start()
    sq_ref[...] = jnp.zeros_like(sq_ref)
    acc_ref[...] = jnp.zeros_like(acc_ref)
    group = 2 if chunks % 2 == 0 else 1
    tile = min(512, acc_ref.shape[2])

    @pl.loop(0, code_ref.shape[1] // 128)
    def _(b):
        cols = pl.ds(pl.multiple_of(b * 128, 128), 128)
        restored = decode(code_ref[:, cols], dec_ref[:, cols], had_ref[...])
        squared = restored * restored
        sq_ref[0] += squared[:half]
        sq_ref[1] += squared[half:]
        x_ref[:, cols] = (restored * gain_ref[:, cols]).astype(jnp.bfloat16)

    pl.semaphore_wait(barrier, (z > 0).astype(jnp.int32) + (z < n - 1).astype(jnp.int32))

    place = (n - 1 - z, z)
    after = (z - 1, z + 1)
    before = (z + 1, z - 1)

    def sum_copy(d, c):
        return pltpu.make_async_remote_copy(
            src_ref=p_ref.at[d, c], dst_ref=r_ref.at[d, c], send_sem=rs_send.at[d, c], recv_sem=rs_recv.at[d, c],
            device_id={"request": after[d]}, device_id_type=MESH)

    def square_copy(d):
        return pltpu.make_async_remote_copy(
            src_ref=sq_ref.at[d], dst_ref=sqr_ref.at[d], send_sem=sq_send.at[d], recv_sem=sq_recv.at[d],
            device_id={"request": after[d]}, device_id_type=MESH)

    def hidden_copy(d, c):
        part = h_ref.at[pl.ds(d * half, half), pl.ds(pl.multiple_of(c * cw, cw), cw)]
        return pltpu.make_async_remote_copy(
            src_ref=part, dst_ref=part, send_sem=ag_send.at[d, c], recv_sem=ag_recv.at[d, c],
            device_id={"request": before[d]}, device_id_type=MESH)

    @pl.loop(0, chunks + 2 * (n - 1) * LAG)
    def _(s):
        @pl.when(s < chunks)
        def _():
            slot = lax.rem(s, 2)

            @pl.when(s + 1 < chunks)
            def _():
                for copy in weights(s + 1, 1 - slot):
                    copy.start()

            for copy in weights(s, slot):
                copy.wait()
            total = jnp.dot(x_ref[...], w_ref[slot], preferred_element_type=jnp.float32).astype(jnp.bfloat16)
            p_ref[0, s] = total[:half]
            p_ref[1, s] = total[half:]

        for d in (0, 1):
            pos = place[d]
            c = s - pos * LAG

            @pl.when((c >= 0) & (c < chunks))
            def _(d=d, pos=pos, c=c):
                @pl.when(c == 0)
                def _():
                    @pl.when(pos > 0)
                    def _():
                        square_copy(d).wait_recv()
                        sq_ref[d] += sqr_ref[d]

                    @pl.when(pos < n - 1)
                    def _():
                        square_copy(d).start()

                    @pl.when(pos == n - 1)
                    def _():
                        total = jnp.sum(sq_ref[d], axis=1, keepdims=True)
                        sq_ref[d] = jnp.broadcast_to(lax.rsqrt(total / D + 1e-05), sq_ref.shape[1:])

                @pl.when(pos > 0)
                def _():
                    sum_copy(d, c).wait_recv()
                    p_ref[d, c] = (p_ref[d, c].astype(jnp.float32) + r_ref[d, c].astype(jnp.float32)).astype(jnp.bfloat16)

                @pl.when(pos < n - 1)
                def _():
                    sum_copy(d, c).start()

                @pl.when(pos == n - 1)
                def _():
                    cols = pl.multiple_of(c * cw, cw)
                    for low in range(0, cw, 128):
                        factor = sq_ref[d]
                        gate = p_ref[d, c, :, low:low + 128].astype(jnp.float32) * factor
                        up = p_ref[d, c, :, cw + low:cw + low + 128].astype(jnp.float32) * factor
                        value = gate / (1.0 + jnp.exp(-gate)) * up
                        h_ref[pl.ds(d * half, half), pl.ds(pl.multiple_of(cols + low, 128), 128)] = value.astype(jnp.bfloat16)
                    hidden_copy(d, c).start()

            back = s - (2 * (n - 1) - pos) * LAG

            @pl.when((pos < n - 1) & (back >= 0) & (back < chunks))
            def _(d=d, pos=pos, back=back):
                hidden_copy(d, back).wait_recv()

                @pl.when(pos > 0)
                def _():
                    hidden_copy(d, back).start()

        @pl.when(s == (n - 1) * LAG)
        def _():
            down_copy.wait()

        for d in (0, 1):
            back = s - (2 * (n - 1) - place[d]) * LAG

            @pl.when((back >= 0) & (back < chunks) & (lax.rem(back, group) == group - 1))
            def _(d=d, back=back):
                units = pl.ds(pl.multiple_of((back - (group - 1)) * cw, cw), group * cw)
                part = h_ref[pl.ds(d * half, half), units]

                @pl.loop(0, acc_ref.shape[2] // tile)
                def _(i):
                    cols = pl.ds(pl.multiple_of(i * tile, tile), tile)
                    acc_ref[d, :, cols] += jnp.dot(part, down_held[units, cols], preferred_element_type=jnp.float32)

    @pl.loop(0, acc_ref.shape[2] // 128)
    def _(b):
        cols = pl.ds(pl.multiple_of(b * 128, 128), 128)
        for d in (0, 1):
            o_ref[pl.ds(d * half, half), cols] = encode(acc_ref[d, :, cols], sign_ref[:, cols], scale_ref[:, cols], had_ref[...])

    for d in (0, 1):
        pos = place[d]

        @pl.when(pos < n - 1)
        def _(d=d):
            square_copy(d).wait_send()

            @pl.loop(0, chunks)
            def _(c):
                sum_copy(d, c).wait_send()

        @pl.when(pos > 0)
        def _(d=d):
            @pl.loop(0, chunks)
            def _(c):
                hidden_copy(d, c).wait_send()


def ffn(n, code, dec, gain, had, sign, scale, gate_weight, up_weight, down_weight):
    rows, depth = code.shape
    units = gate_weight.shape[1]
    cw = 128
    chunks = units // cw
    half = rows // 2
    vmem = pl.BlockSpec(memory_space=pltpu.VMEM)
    return pl.pallas_call(
        functools.partial(ffn_body, n, chunks, cw),
        out_shape=jax.ShapeDtypeStruct((rows, down_weight.shape[1]), jnp.bfloat16),
        in_specs=[vmem] * 6 + [pl.BlockSpec(memory_space=pl.ANY)] * 3,
        out_specs=vmem,
        scratch_shapes=[
            pltpu.VMEM((rows, units), jnp.bfloat16),
            pltpu.VMEM(down_weight.shape, jnp.bfloat16),
            pltpu.VMEM((2, half, down_weight.shape[1]), jnp.float32),
            pltpu.SemaphoreType.DMA,
            pltpu.VMEM((rows, depth), jnp.bfloat16),
            pltpu.VMEM((2, half, 128), jnp.float32),
            pltpu.VMEM((2, half, 128), jnp.float32),
            pltpu.VMEM((2, depth, 2 * cw), jnp.bfloat16),
            pltpu.VMEM((2, chunks, half, 2 * cw), jnp.bfloat16),
            pltpu.VMEM((2, chunks, half, 2 * cw), jnp.bfloat16),
            pltpu.SemaphoreType.DMA((2, 2)),
            pltpu.SemaphoreType.DMA((2, chunks)),
            pltpu.SemaphoreType.DMA((2, chunks)),
            pltpu.SemaphoreType.DMA((2, chunks)),
            pltpu.SemaphoreType.DMA((2, chunks)),
            pltpu.SemaphoreType.DMA((2,)),
            pltpu.SemaphoreType.DMA((2,)),
        ],
        compiler_params=pltpu.CompilerParams(collective_id=0, has_side_effects=True, vmem_limit_bytes=VMEM_LIMIT),
    )(code, dec, gain, had, sign, scale, gate_weight, up_weight, down_weight)


def shards(n_tensor, n_request, attn_heads, out_weight, resid, gain, gate_weight, up_weight, down_weight, signs, expos):
    had = hadamard()
    sign = (2 * signs - 1).astype(jnp.float32)
    shift = expos + jnp.array([[4], [8], [4], [6]], jnp.int32)
    enc = jnp.repeat(0.125 * jnp.exp2(-shift.astype(jnp.float32)), 128, axis=1)
    dec = jnp.repeat(0.0625 * jnp.exp2(shift.astype(jnp.float32)), 128, axis=1) * sign
    row = lambda table, k: table[k:k + 1]

    coded = project(attn_heads, out_weight, row(sign, 0), row(enc, 0), had)
    hidden_state, gathered = exchange(n_tensor, True, 1, coded, resid, row(dec, 0), row(sign, 1), row(enc, 1), had)
    coded = ffn(
        n_request, gathered, row(dec, 1), gain.astype(jnp.float32)[None, :], had, row(sign, 2), row(enc, 2),
        gate_weight, up_weight, down_weight)
    (gathered,) = exchange(n_tensor, False, 2, coded, hidden_state, row(dec, 2), row(sign, 3), row(enc, 3), had)
    return finish(gathered, row(dec, 3), had)


def solution(mesh):
    return jax.shard_map(
        functools.partial(shards, mesh.shape["tensor"], mesh.shape["request"]),
        mesh=mesh,
        in_specs=(
            P("parts", "tensor"),
            P("tensor", "request"),
            P(("parts", "tensor"), "request"),
            P("request"),
            P("request", "tensor"),
            P("request", "tensor"),
            P("tensor", "request"),
            P(None, "request"),
            P(None, "request"),
        ),
        out_specs=P("parts", "request"),
        check_vma=False,
    )
```

```python
import functools

import jax
import jax.numpy as jnp
from jax import lax
from jax.experimental import pallas as pl
from jax.experimental.pallas import tpu as pltpu
from jax.sharding import PartitionSpec as P

D = 8192
MESH = pl.DeviceIdType.MESH
LAG = 2
VMEM_LIMIT = 52 * 2**20


def hadamard():
    index = jnp.arange(128, dtype=jnp.int32)
    common = jnp.bitwise_and(index[:, None], index[None, :])
    ones_count = jnp.zeros((128, 128), jnp.int32)
    for level in range(7):
        ones_count = ones_count + jnp.bitwise_and(jnp.right_shift(common, level), 1)
    return (1 - 2 * (ones_count % 2)).astype(jnp.bfloat16)


def turn(values, had):
    high = values.astype(jnp.bfloat16)
    low = (values - high.astype(jnp.float32)).astype(jnp.bfloat16)
    return jnp.dot(high, had, preferred_element_type=jnp.float32) + jnp.dot(low, had, preferred_element_type=jnp.float32)


def encode(values, sign, scale, had):
    return jnp.clip(turn(values * sign, had) * scale, -448.0, 448.0).astype(jnp.bfloat16)


def decode(codes, scale, had):
    return jnp.dot(codes, had, preferred_element_type=jnp.float32) * scale


def exchange_body(nx, parts, keep, *refs):
    if keep:
        a_ref, w_ref, first_sign, first_scale, *refs = refs
    else:
        code_ref, *refs = refs
    base_ref, dec_ref, sign_ref, scale_ref, had_ref, *refs = refs
    if keep:
        state_ref, *refs = refs
        *refs, code_ref, w_held, w_sem = refs
    (o_ref, s_ref, q_ref, g_ref, pair_send, pair_recv, sum_send, sum_recv, out_send, out_recv, fwd_send, fwd_recv) = refs
    t = lax.axis_index("tensor")
    core = lax.rem(t, 2)
    chip = t // 2
    width = code_ref.shape[3] // parts
    sibling = chip * 2 + 1 - core

    def chip_at(k):
        return lax.rem(chip + k + nx, nx)

    def span(j):
        return slice(j * width, (j + 1) * width)

    def cols(j):
        return pl.ds(j * width, width)

    def pair_copy(j):
        return pltpu.make_async_remote_copy(
            src_ref=code_ref.at[:, 1 - core, :, cols(j)], dst_ref=s_ref.at[:, :, cols(j)],
            send_sem=pair_send.at[j], recv_sem=pair_recv.at[j],
            device_id={"tensor": sibling}, device_id_type=MESH)

    def sum_copy(k, j):
        return pltpu.make_async_remote_copy(
            src_ref=q_ref.at[chip_at(k), :, cols(j)], dst_ref=g_ref.at[k - 1, :, cols(j)],
            send_sem=sum_send.at[k - 1, j], recv_sem=sum_recv.at[k - 1, j],
            device_id={"tensor": chip_at(k) * 2 + core}, device_id_type=MESH)

    def out_copy(k, j):
        part = o_ref.at[chip, core, :, cols(j)]
        return pltpu.make_async_remote_copy(
            src_ref=part, dst_ref=part, send_sem=out_send.at[k - 1, j], recv_sem=out_recv.at[k - 1, j],
            device_id={"tensor": chip_at(k) * 2 + core}, device_id_type=MESH)

    def forward_copy(k, j):
        part = o_ref.at[chip_at(-k), core, :, cols(j)]
        return pltpu.make_async_remote_copy(
            src_ref=part, dst_ref=part, send_sem=fwd_send.at[k, j], recv_sem=fwd_recv.at[k, j],
            device_id={"tensor": sibling}, device_id_type=MESH)

    def weight_copy(j):
        return pltpu.make_async_copy(w_ref.at[:, cols(j)], w_held.at[:, cols(j)], w_sem.at[j])

    def produce(j):
        weight_copy(j).wait()
        tile = min(width, 256)
        own = code_ref.shape[2]

        @pl.loop(0, width // tile)
        def _(i):
            start = pl.multiple_of(j * width + i * tile, 128)
            product = jnp.dot(a_ref[...], w_held[:, pl.ds(start, tile)], preferred_element_type=jnp.float32)
            for low in range(0, tile, 128):
                here = pl.ds(pl.multiple_of(start + low, 128), 128)
                turned = turn(product[:, low:low + 128] * first_sign[:, here], had_ref[...]) * first_scale[:, here]
                turned = jnp.clip(turned, -448.0, 448.0)
                for to in range(2 * nx):
                    code_ref[to // 2, to % 2, :, here] = turned[to * own:(to + 1) * own].astype(jnp.bfloat16)

    if keep:
        for j in range(parts):
            weight_copy(j).start()
    barrier = pltpu.get_barrier_semaphore()
    pl.semaphore_signal(barrier, inc=1, device_id={"tensor": sibling}, device_id_type=MESH)
    for k in range(1, nx):
        pl.semaphore_signal(barrier, inc=1, device_id={"tensor": chip_at(k) * 2 + core}, device_id_type=MESH)
    pl.semaphore_wait(barrier, nx)

    def add_pair(j):
        pair_copy(j).wait_recv()
        for chip_to in range(nx):
            both = code_ref[chip_to, core, :, span(j)].astype(jnp.float32) + s_ref[chip_to, :, span(j)].astype(jnp.float32)
            q_ref[chip_to, :, span(j)] = both.astype(jnp.bfloat16)
        for k in range(1, nx):
            sum_copy(k, j).start()

    for j in range(parts):
        if keep:
            produce(j)
        pair_copy(j).start()
        if j > 0:
            add_pair(j - 1)
    add_pair(parts - 1)
    for j in range(parts):
        total = q_ref[chip, :, span(j)].astype(jnp.float32)
        for k in range(1, nx):
            sum_copy(k, j).wait_recv()
            total += g_ref[k - 1, :, span(j)].astype(jnp.float32)
        total = total.astype(jnp.bfloat16)
        for low in range(0, width, 128):
            here = slice(j * width + low, j * width + low + 128)
            state = base_ref[:, here].astype(jnp.float32) + decode(total[:, low:low + 128], dec_ref[:, here], had_ref[...])
            if keep:
                state_ref[:, here] = state
            o_ref[chip, core, :, here] = encode(state, sign_ref[:, here], scale_ref[:, here], had_ref[...])
        for k in range(1, nx):
            out_copy(k, j).start()
        forward_copy(0, j).start()
    for j in range(parts):
        for k in range(1, nx):
            out_copy(k, j).wait_recv()
            forward_copy(k, j).start()
    for j in range(parts):
        pair_copy(j).wait_send()
        for k in range(nx):
            forward_copy(k, j).wait()
        for k in range(1, nx):
            sum_copy(k, j).wait_send()
            out_copy(k, j).wait_send()


def exchange(n_tensor, keep, name, first, base, dec, sign, scale, had):
    rows, width = first[0].shape[0], base.shape[1]
    nx, own, parts = n_tensor // 2, rows // n_tensor, 4
    vmem = pl.BlockSpec(memory_space=pltpu.VMEM)
    states = [jax.ShapeDtypeStruct((own, width), jnp.float32)] if keep else []
    *state, out = pl.pallas_call(
        functools.partial(exchange_body, nx, parts, keep),
        out_shape=states + [jax.ShapeDtypeStruct((nx, 2, own, width), jnp.bfloat16)],
        in_specs=([vmem, pl.BlockSpec(memory_space=pl.ANY), vmem, vmem] if keep else [vmem]) + [vmem] * 5,
        out_specs=[vmem] * (len(states) + 1),
        scratch_shapes=[
            pltpu.VMEM((nx, own, width), jnp.bfloat16),
            pltpu.VMEM((nx, own, width), jnp.bfloat16),
            pltpu.VMEM((nx - 1, own, width), jnp.bfloat16),
            pltpu.SemaphoreType.DMA((parts,)),
            pltpu.SemaphoreType.DMA((parts,)),
            pltpu.SemaphoreType.DMA((nx - 1, parts)),
            pltpu.SemaphoreType.DMA((nx - 1, parts)),
            pltpu.SemaphoreType.DMA((nx - 1, parts)),
            pltpu.SemaphoreType.DMA((nx - 1, parts)),
            pltpu.SemaphoreType.DMA((nx, parts)),
            pltpu.SemaphoreType.DMA((nx, parts)),
        ] + ([
            pltpu.VMEM((nx, 2, own, width), jnp.bfloat16),
            pltpu.VMEM(first[1].shape, jnp.bfloat16),
            pltpu.SemaphoreType.DMA((parts,)),
        ] if keep else []),
        compiler_params=pltpu.CompilerParams(collective_id=name, has_side_effects=True, vmem_limit_bytes=VMEM_LIMIT),
    )(*(first if keep else [first[0].reshape(nx, 2, own, width)]), base, dec, sign, scale, had)
    return (*state, out.reshape(rows, width))


def finish_body(code_ref, dec_ref, had_ref, o_ref):
    for low in range(0, code_ref.shape[1], 128):
        cols = slice(low, low + 128)
        o_ref[:, cols] = decode(code_ref[:, cols], dec_ref[:, cols], had_ref[...]).astype(jnp.bfloat16)


def finish(code, dec, had):
    rows, width = code.shape
    block = min(width, 512)
    return pl.pallas_call(
        finish_body,
        grid=(width // block,),
        in_specs=[
            pl.BlockSpec((rows, block), lambda j: (0, j)),
            pl.BlockSpec((1, block), lambda j: (0, j)),
            pl.BlockSpec((128, 128), lambda j: (0, 0)),
        ],
        out_specs=pl.BlockSpec((rows, block), lambda j: (0, j)),
        out_shape=jax.ShapeDtypeStruct((rows, width), jnp.bfloat16),
        compiler_params=pltpu.CompilerParams(vmem_limit_bytes=VMEM_LIMIT),
    )(code, dec, had)


def ffn_body(n, chunks, cw, code_ref, dec_ref, gain_ref, had_ref, sign_ref, scale_ref, gate_ref, up_ref, down_ref, o_ref,
             h_ref, down_held, acc_ref, down_sem, x_ref, sq_ref, sqr_ref, w_ref, p_ref, r_ref,
             w_sem, rs_send, rs_recv, ag_send, ag_recv, sq_send, sq_recv):
    z = lax.axis_index("request")
    half = p_ref.shape[2]

    def weights(c, slot):
        cols = pl.ds(pl.multiple_of(c * cw, cw), cw)
        return (
            pltpu.make_async_copy(gate_ref.at[:, cols], w_ref.at[slot, :, pl.ds(0, cw)], w_sem.at[slot, 0]),
            pltpu.make_async_copy(up_ref.at[:, cols], w_ref.at[slot, :, pl.ds(cw, cw)], w_sem.at[slot, 1]),
        )

    barrier = pltpu.get_barrier_semaphore()

    @pl.when(z > 0)
    def _():
        pl.semaphore_signal(barrier, inc=1, device_id={"request": z - 1}, device_id_type=MESH)

    @pl.when(z < n - 1)
    def _():
        pl.semaphore_signal(barrier, inc=1, device_id={"request": z + 1}, device_id_type=MESH)

    for copy in weights(0, 0):
        copy.start()

    down_copy = pltpu.make_async_copy(down_ref, down_held, down_sem)
    down_copy.start()
    sq_ref[...] = jnp.zeros_like(sq_ref)
    acc_ref[...] = jnp.zeros_like(acc_ref)
    group = 2 if chunks % 2 == 0 else 1
    tile = min(512, acc_ref.shape[2])

    @pl.loop(0, code_ref.shape[1] // 128)
    def _(b):
        cols = pl.ds(pl.multiple_of(b * 128, 128), 128)
        restored = decode(code_ref[:, cols], dec_ref[:, cols], had_ref[...])
        squared = restored * restored
        sq_ref[0] += squared[:half]
        sq_ref[1] += squared[half:]
        x_ref[:, cols] = (restored * gain_ref[:, cols]).astype(jnp.bfloat16)

    pl.semaphore_wait(barrier, (z > 0).astype(jnp.int32) + (z < n - 1).astype(jnp.int32))

    place = (n - 1 - z, z)
    after = (z - 1, z + 1)
    before = (z + 1, z - 1)

    def sum_copy(d, c):
        return pltpu.make_async_remote_copy(
            src_ref=p_ref.at[d, c], dst_ref=r_ref.at[d, c], send_sem=rs_send.at[d, c], recv_sem=rs_recv.at[d, c],
            device_id={"request": after[d]}, device_id_type=MESH)

    def square_copy(d):
        return pltpu.make_async_remote_copy(
            src_ref=sq_ref.at[d], dst_ref=sqr_ref.at[d], send_sem=sq_send.at[d], recv_sem=sq_recv.at[d],
            device_id={"request": after[d]}, device_id_type=MESH)

    def hidden_copy(d, c):
        part = h_ref.at[pl.ds(d * half, half), pl.ds(pl.multiple_of(c * cw, cw), cw)]
        return pltpu.make_async_remote_copy(
            src_ref=part, dst_ref=part, send_sem=ag_send.at[d, c], recv_sem=ag_recv.at[d, c],
            device_id={"request": before[d]}, device_id_type=MESH)

    @pl.loop(0, chunks + 2 * (n - 1) * LAG)
    def _(s):
        @pl.when(s < chunks)
        def _():
            slot = lax.rem(s, 2)

            @pl.when(s + 1 < chunks)
            def _():
                for copy in weights(s + 1, 1 - slot):
                    copy.start()

            for copy in weights(s, slot):
                copy.wait()
            total = jnp.dot(x_ref[...], w_ref[slot], preferred_element_type=jnp.float32).astype(jnp.bfloat16)
            p_ref[0, s] = total[:half]
            p_ref[1, s] = total[half:]

        for d in (0, 1):
            pos = place[d]
            c = s - pos * LAG

            @pl.when((c >= 0) & (c < chunks))
            def _(d=d, pos=pos, c=c):
                @pl.when(c == 0)
                def _():
                    @pl.when(pos > 0)
                    def _():
                        square_copy(d).wait_recv()
                        sq_ref[d] += sqr_ref[d]

                    @pl.when(pos < n - 1)
                    def _():
                        square_copy(d).start()

                    @pl.when(pos == n - 1)
                    def _():
                        total = jnp.sum(sq_ref[d], axis=1, keepdims=True)
                        sq_ref[d] = jnp.broadcast_to(lax.rsqrt(total / D + 1e-05), sq_ref.shape[1:])

                @pl.when(pos > 0)
                def _():
                    sum_copy(d, c).wait_recv()
                    p_ref[d, c] = (p_ref[d, c].astype(jnp.float32) + r_ref[d, c].astype(jnp.float32)).astype(jnp.bfloat16)

                @pl.when(pos < n - 1)
                def _():
                    sum_copy(d, c).start()

                @pl.when(pos == n - 1)
                def _():
                    cols = pl.multiple_of(c * cw, cw)
                    for low in range(0, cw, 128):
                        factor = sq_ref[d]
                        gate = p_ref[d, c, :, low:low + 128].astype(jnp.float32) * factor
                        up = p_ref[d, c, :, cw + low:cw + low + 128].astype(jnp.float32) * factor
                        value = gate / (1.0 + jnp.exp(-gate)) * up
                        h_ref[pl.ds(d * half, half), pl.ds(pl.multiple_of(cols + low, 128), 128)] = value.astype(jnp.bfloat16)
                    hidden_copy(d, c).start()

            back = s - (2 * (n - 1) - pos) * LAG

            @pl.when((pos < n - 1) & (back >= 0) & (back < chunks))
            def _(d=d, pos=pos, back=back):
                hidden_copy(d, back).wait_recv()

                @pl.when(pos > 0)
                def _():
                    hidden_copy(d, back).start()

        @pl.when(s == (n - 1) * LAG)
        def _():
            down_copy.wait()

        for d in (0, 1):
            back = s - (2 * (n - 1) - place[d]) * LAG

            @pl.when((back >= 0) & (back < chunks) & (lax.rem(back, group) == group - 1))
            def _(d=d, back=back):
                units = pl.ds(pl.multiple_of((back - (group - 1)) * cw, cw), group * cw)
                part = h_ref[pl.ds(d * half, half), units]

                @pl.loop(0, acc_ref.shape[2] // tile)
                def _(i):
                    cols = pl.ds(pl.multiple_of(i * tile, tile), tile)
                    acc_ref[d, :, cols] += jnp.dot(part, down_held[units, cols], preferred_element_type=jnp.float32)

    @pl.loop(0, acc_ref.shape[2] // 128)
    def _(b):
        cols = pl.ds(pl.multiple_of(b * 128, 128), 128)
        for d in (0, 1):
            o_ref[pl.ds(d * half, half), cols] = encode(acc_ref[d, :, cols], sign_ref[:, cols], scale_ref[:, cols], had_ref[...])

    for d in (0, 1):
        pos = place[d]

        @pl.when(pos < n - 1)
        def _(d=d):
            square_copy(d).wait_send()

            @pl.loop(0, chunks)
            def _(c):
                sum_copy(d, c).wait_send()

        @pl.when(pos > 0)
        def _(d=d):
            @pl.loop(0, chunks)
            def _(c):
                hidden_copy(d, c).wait_send()


def ffn(n, code, dec, gain, had, sign, scale, gate_weight, up_weight, down_weight):
    rows, depth = code.shape
    units = gate_weight.shape[1]
    cw = 128
    chunks = units // cw
    half = rows // 2
    vmem = pl.BlockSpec(memory_space=pltpu.VMEM)
    return pl.pallas_call(
        functools.partial(ffn_body, n, chunks, cw),
        out_shape=jax.ShapeDtypeStruct((rows, down_weight.shape[1]), jnp.bfloat16),
        in_specs=[vmem] * 6 + [pl.BlockSpec(memory_space=pl.ANY)] * 3,
        out_specs=vmem,
        scratch_shapes=[
            pltpu.VMEM((rows, units), jnp.bfloat16),
            pltpu.VMEM(down_weight.shape, jnp.bfloat16),
            pltpu.VMEM((2, half, down_weight.shape[1]), jnp.float32),
            pltpu.SemaphoreType.DMA,
            pltpu.VMEM((rows, depth), jnp.bfloat16),
            pltpu.VMEM((2, half, 128), jnp.float32),
            pltpu.VMEM((2, half, 128), jnp.float32),
            pltpu.VMEM((2, depth, 2 * cw), jnp.bfloat16),
            pltpu.VMEM((2, chunks, half, 2 * cw), jnp.bfloat16),
            pltpu.VMEM((2, chunks, half, 2 * cw), jnp.bfloat16),
            pltpu.SemaphoreType.DMA((2, 2)),
            pltpu.SemaphoreType.DMA((2, chunks)),
            pltpu.SemaphoreType.DMA((2, chunks)),
            pltpu.SemaphoreType.DMA((2, chunks)),
            pltpu.SemaphoreType.DMA((2, chunks)),
            pltpu.SemaphoreType.DMA((2,)),
            pltpu.SemaphoreType.DMA((2,)),
        ],
        compiler_params=pltpu.CompilerParams(collective_id=0, has_side_effects=True, vmem_limit_bytes=VMEM_LIMIT),
    )(code, dec, gain, had, sign, scale, gate_weight, up_weight, down_weight)


def shards(n_tensor, n_request, attn_heads, out_weight, resid, gain, gate_weight, up_weight, down_weight, signs, expos):
    had = hadamard()
    sign = (2 * signs - 1).astype(jnp.float32)
    shift = expos + jnp.array([[4], [8], [4], [6]], jnp.int32)
    enc = jnp.repeat(0.125 * jnp.exp2(-shift.astype(jnp.float32)), 128, axis=1)
    dec = jnp.repeat(0.0625 * jnp.exp2(shift.astype(jnp.float32)), 128, axis=1) * sign
    row = lambda table, k: table[k:k + 1]

    first = (attn_heads, out_weight, row(sign, 0), row(enc, 0))
    hidden_state, gathered = exchange(n_tensor, True, 1, first, resid, row(dec, 0), row(sign, 1), row(enc, 1), had)
    coded = ffn(
        n_request, gathered, row(dec, 1), gain.astype(jnp.float32)[None, :], had, row(sign, 2), row(enc, 2),
        gate_weight, up_weight, down_weight)
    (gathered,) = exchange(n_tensor, False, 2, (coded,), hidden_state, row(dec, 2), row(sign, 3), row(enc, 3), had)
    return finish(gathered, row(dec, 3), had)


def solution(mesh):
    return jax.shard_map(
        functools.partial(shards, mesh.shape["tensor"], mesh.shape["request"]),
        mesh=mesh,
        in_specs=(
            P("parts", "tensor"),
            P("tensor", "request"),
            P(("parts", "tensor"), "request"),
            P("request"),
            P("request", "tensor"),
            P("request", "tensor"),
            P("tensor", "request"),
            P(None, "request"),
            P(None, "request"),
        ),
        out_specs=P("parts", "request"),
        check_vma=False,
    )
```
